256 devices in a mesh: band: 8 (over x, core), dom: 32 (over z, y).
Axes of the slice: x: 4, y: 4, z: 8, core: 2. Of those that a mesh axis runs over, the one named last changes fastest.
Arguments:
- orbitals: bfloat16 [256, 192, 48, 64], P('band', 'dom'), may hold values from -1.796875 to 1.796875
- potential: float32 [192, 48, 64], P('dom'), may hold values from -2 to 1
- projectors: float32 [2048, 128], P('dom'), may hold values from -1.5 to 1.5
- coupling: float32 [1024], P('dom'), may hold values from 0.5 to 2
- slot_block: int32 [2048], P('dom'), may hold values from 0 to 143
- slot_projector: int32 [2048], P('dom'), may hold values from 0 to 1023, as said below
- slot_count: int32 [32], P('dom'), may hold values from 16 to 64, as said below
- locked: bfloat16 [2048, 192, 3072], P(None, 'dom', 'band'), may hold values from -0.0078125 to 0.0078125
Outputs:
- orthogonal: bfloat16 [256, 192, 3072], P(None, 'dom', 'band')
- margins: float32 [2048, 256], P(('band', 'dom'))
The draws below stay inside these ranges and needn't reach their ends.
Inputs may be any that keep to these rules, and one draw needn't show every extreme that they name: `slot_projector`: projector p belongs to domain p // 32; a slot of domain d names a projector of domain d - 1, d or d + 1, cyclically; slot 0 of every domain names one of domain d - 1 and slot 1 one of domain d + 1. The used slots of a domain are its first slot_count slots; some domain uses all and some uses 64 // 4.
All inputs are finite; a program needn't handle non-finite values.
Results may differ from the reference program's by a relative error of at most 0.0039.
The reference program's roundings to bfloat16 on the way (of `residual` and `coeffs`) count: a program that leaves them out, or rounds other values in their place, can miss the bound.
Values may be sent and summed in bfloat16 or wider, within the bound.
No kernel may reach another device: no remote copies, remote signals or barrier semaphores. Data moves between devices by JAX's collectives and lax.ppermute only.
A program may use at most 320 MiB of HBM per device.

```python
import jax
import jax.numpy as jnp
from jax import lax

BANDS_GRP = 32
LOCKED = 2048
CX = 6
NZ = 48
NY = 64
BS = 128
SLOTS = 64
PROJ_DOM = 32
BANDS = 256
NX = 192
PLANE = 3072
NB = 144
NPROJ = 1024
N_BAND = 8
N_DOM = 32


def draw_slot_projector(key, part):
    key = jax.random.fold_in(key, 11)
    key_shift, key_local = jax.random.split(key)
    position = jnp.arange(N_DOM * SLOTS, dtype=jnp.int32)
    domain = position // SLOTS
    within = position % SLOTS
    shift = jax.random.randint(key_shift, (N_DOM * SLOTS,), -1, 2, dtype=jnp.int32)
    local_id = jax.random.randint(key_local, (N_DOM * SLOTS,), 0, PROJ_DOM, dtype=jnp.int32)
    shift = jnp.where(within == 0, -1, shift)
    shift = jnp.where(within == 1, 1, shift)
    local_id = jnp.where(position == 0, PROJ_DOM - 1, local_id)
    local_id = jnp.where(position == SLOTS, 0, local_id)
    return ((domain + shift + N_DOM) % N_DOM * PROJ_DOM + local_id).astype(jnp.int32)


def draw_slot_count(key, part):
    key = jax.random.fold_in(key, 23)
    key_count, key_order = jax.random.split(key)
    counts = jax.random.randint(key_count, (N_DOM,), SLOTS // 4, SLOTS + 1, dtype=jnp.int32)
    ranking = jax.random.permutation(key_order, N_DOM)
    counts = jnp.where(ranking == 0, SLOTS, counts)
    counts = jnp.where(ranking == 1, SLOTS // 4, counts)
    return counts.astype(jnp.int32)


def set_ends(entries, stream_key, least, top_value):
    dims = entries.shape
    index_at = [jax.random.randint(jax.random.fold_in(stream_key, axis), (), 0, dims[axis]) for axis in range(len(dims))]
    entries = entries.at[tuple(index_at)].set(least)
    longest = dims.index(max(dims))
    index_at[longest] = (index_at[longest] + 1) % dims[longest]
    return entries.at[tuple(index_at)].set(top_value)


def levels(rng, extent, cuts, least, largest):
    loudness, own = 1.0, jax.random.fold_in(rng, 6)
    for dim, parts in cuts:
        draws = jnp.exp(jax.random.uniform(jax.random.fold_in(own, dim), (parts,), jnp.float32, least / len(cuts), largest / len(cuts)))
        loudness = loudness * jnp.repeat(draws, extent[dim] // parts).reshape([-1 if axis == dim else 1 for axis in range(len(extent))])
    return loudness


def normal_values(own_key, extent, spread, most, cuts=(), kind=jnp.bfloat16):
    values = spread * jax.random.normal(own_key, extent, jnp.float32)
    if cuts:
        values = values * levels(own_key, extent, cuts, -0.22, 0.18)
    return jnp.clip(values, -most, most).astype(kind)


def setup_inputs(seed: int = 0) -> dict:
    streams_of = jax.random.split(jax.random.key(seed), 9)
    return {
        "orbitals": normal_values(streams_of[0], (BANDS, NX, NZ, NY), 0.3, 1.796875, ((0, 8), (1, 32))),
        "potential": jnp.clip(-2.0 + 3.0 * jax.random.uniform(streams_of[1], (NX, NZ, NY), jnp.float32) ** levels(streams_of[1], (NX, NZ, NY), ((0, 32),), -0.2, 0.2), -2.0, 1.0),
        "projectors": normal_values(streams_of[2], (NPROJ * SLOTS // PROJ_DOM, BS), (BS // 8) ** -0.5, 1.5, ((0, 32),), jnp.float32),
        "coupling": jnp.clip(0.5 + 1.5 * jax.random.uniform(streams_of[3], (NPROJ,), jnp.float32) ** levels(streams_of[3], (NPROJ,), ((0, 32),), -0.2, 0.2), 0.5, 2.0),
        "slot_block": set_ends(jax.random.randint(streams_of[4], (NPROJ * SLOTS // PROJ_DOM,), 0, NB), jax.random.fold_in(streams_of[4], 1), 0, NB - 1).astype(jnp.int32),
        "slot_projector": draw_slot_projector(jax.random.fold_in(streams_of[8], 71), 0),
        "slot_count": draw_slot_count(jax.random.fold_in(streams_of[8], 71), 0),
        "locked": normal_values(streams_of[7], (LOCKED, NX, PLANE), (NX * PLANE) ** -0.5, 0.0078125, ((1, 32), (2, 8))),
    }


COEFFS = (-5369.0 / 1800.0, 12.0 / 7.0, -15.0 / 56.0, 10.0 / 189.0, -1.0 / 112.0, 2.0 / 825.0, -1.0 / 5544.0)


def laplacian(orbital, extended):
    planes_x = orbital.shape[1]
    depth_z = orbital.shape[2]
    laplace = 3.0 * COEFFS[0] * orbital
    padded = jnp.pad(orbital, ((0, 0), (0, 0), (6, 6), (0, 0)))
    for offset in range(1, 7):
        weight = COEFFS[offset]
        laplace = laplace + weight * (extended[:, 6 + offset:6 + offset + planes_x] + extended[:, 6 - offset:6 - offset + planes_x])
        laplace = laplace + weight * (jnp.roll(orbital, offset, 3) + jnp.roll(orbital, -offset, 3))
        laplace = laplace + weight * (padded[:, :, 6 + offset:6 + offset + depth_z] + padded[:, :, 6 - offset:6 - offset + depth_z])
    return laplace


def residual_group(group, potential, projectors, coupling, slot_block, slot_projector, slot_count):
    orbital = group.astype(jnp.float32)
    extended = jnp.concatenate([orbital[:, -6:], orbital, orbital[:, :6]], axis=1)
    laplace = laplacian(orbital, extended)
    flat = orbital.reshape(BANDS_GRP, N_DOM, NB, BS)
    blocks_index = slot_block.reshape(N_DOM, SLOTS)
    domain_index = jnp.broadcast_to(jnp.arange(N_DOM, dtype=jnp.int32)[:, None], (N_DOM, SLOTS))
    blocks = flat[:, domain_index, blocks_index]
    shaped = projectors.reshape(N_DOM, SLOTS, BS)
    active = (jnp.arange(SLOTS, dtype=jnp.int32)[None, :] < slot_count[:, None]).astype(jnp.float32)
    inner_part = jnp.sum(blocks * shaped[None], axis=3) * active[None]
    partial_value = jax.ops.segment_sum(inner_part.reshape(BANDS_GRP, -1).T, slot_projector, num_segments=PROJ_DOM * N_DOM).T
    table = partial_value * coupling[None]
    slot_value = table[:, slot_projector].reshape(BANDS_GRP, N_DOM, SLOTS) * active[None]
    contribution = slot_value[..., None] * shaped[None]
    nonlocal_term = jnp.zeros_like(flat).at[:, domain_index, blocks_index].add(contribution).reshape(orbital.shape)
    hamilton = -0.5 * laplace + potential[None] * orbital + nonlocal_term
    numerator = jnp.sum(orbital * hamilton, axis=(1, 2, 3))
    denominator = jnp.sum(orbital * orbital, axis=(1, 2, 3))
    energy = numerator / denominator
    return (hamilton - energy[:, None, None, None] * orbital).astype(jnp.bfloat16)


def reference(orbitals, potential, projectors, coupling, slot_block, slot_projector, slot_count, locked):
    grouped = orbitals.reshape(N_BAND, BANDS_GRP, NX, NZ, NY)
    residual = lax.map(lambda group: residual_group(group, potential, projectors, coupling, slot_block, slot_projector, slot_count), grouped)
    residual = residual.reshape(BANDS_GRP * N_BAND, NX, NZ * NY)

    def accumulate(total, domain):
        locked_part = lax.dynamic_slice_in_dim(locked, domain * CX, CX, 1).astype(jnp.float32).reshape(LOCKED, -1)
        residual_part = lax.dynamic_slice_in_dim(residual, domain * CX, CX, 1).astype(jnp.float32).reshape(BANDS_GRP * N_BAND, -1)
        return total + jnp.dot(locked_part, residual_part.T, precision=lax.Precision.HIGHEST), None

    summed, _ = lax.scan(accumulate, jnp.zeros((LOCKED, BANDS_GRP * N_BAND), jnp.float32), jnp.arange(N_DOM, dtype=jnp.int32))
    coeffs = lax.optimization_barrier(summed.astype(jnp.bfloat16)).astype(jnp.float32)

    def cleaned(domain):
        locked_part = lax.dynamic_slice_in_dim(locked, domain * CX, CX, 1).astype(jnp.float32).reshape(LOCKED, -1)
        residual_part = lax.dynamic_slice_in_dim(residual, domain * CX, CX, 1).astype(jnp.float32).reshape(BANDS_GRP * N_BAND, -1)
        result = residual_part - jnp.dot(coeffs.T, locked_part, precision=lax.Precision.HIGHEST)
        return result.astype(jnp.bfloat16).reshape(BANDS_GRP * N_BAND, CX, NZ * NY)

    pieces = lax.map(cleaned, jnp.arange(N_DOM, dtype=jnp.int32))
    orthogonal = jnp.transpose(pieces, (1, 0, 2, 3)).reshape(BANDS_GRP * N_BAND, NX, NZ * NY)
    return orthogonal, summed
```

```python
import functools

import jax
import jax.numpy as jnp
import numpy as np
from jax import lax
from jax.experimental import pallas as pl
from jax.experimental.pallas import tpu as pltpu
from jax.sharding import Mesh
from jax.sharding import PartitionSpec as P

BS = 128
CHUNKS = 1

COEFFS = (
    -5369.0 / 1800.0,
    12.0 / 7.0,
    -15.0 / 56.0,
    10.0 / 189.0,
    -1.0 / 112.0,
    2.0 / 825.0,
    -1.0 / 5544.0,
)
HALF = tuple(-0.5 * c for c in COEFFS)
WIDTH = 6
DOM = ("z", "y")
BAND = ("x", "core")
F32 = jnp.float32
BF16 = jnp.bfloat16
VMEM = pl.BlockSpec(memory_space=pltpu.VMEM)
SMEM = pl.BlockSpec(memory_space=pltpu.SMEM)


def params(mib):
    return pltpu.CompilerParams(vmem_limit_bytes=mib * 1024 * 1024)


@functools.lru_cache
def plane_weights(width_y):
    src = np.arange(1024)
    dst = np.arange(256)
    dz = np.abs((src // width_y - 2 * (384 // (2 * width_y)))[:, None] - (dst // width_y)[None])
    dy = np.abs((src % width_y)[:, None] - (dst % width_y)[None])
    dy = np.minimum(dy, width_y - dy)
    table = np.zeros(2048)
    table[1 : WIDTH + 1] = HALF[1:]
    full = np.where(dy == 0, table[dz], 0.0) + np.where(dz == 0, table[dy], 0.0)
    terms = []
    for _ in range(3):
        term = full.astype(np.float32).astype(BF16)
        terms.append(term)
        full = full - term.astype(np.float64)
    return np.stack(terms)


def inner_kernel(block_ref, x_ref, proj_ref, onehot_ref, out_ref):
    rows = x_ref.shape[0]
    slots = proj_ref.shape[0]
    lane = lax.broadcasted_iota(jnp.int32, (rows, BS), 1)

    def body(s, acc):
        start = pl.multiple_of(block_ref[s] * BS, BS)
        cells = x_ref[:, pl.ds(start, BS)].astype(F32)
        total = jnp.sum(cells * proj_ref[pl.ds(s, 1), :], axis=1, keepdims=True)
        return jnp.where(lane == s, total, acc)

    acc = lax.fori_loop(0, slots, body, jnp.zeros((rows, BS), F32), unroll=8)
    out_ref[...] = jnp.dot(
        acc, onehot_ref[...], precision=lax.Precision.HIGHEST, preferred_element_type=F32
    )


def local_kernel(planes, x_ref, pot_ref, w_ref, out_ref, pad_ref):
    rows = x_ref.shape[0]
    plane = x_ref.shape[1] // planes
    zeros = jnp.zeros((planes * rows, 384), BF16)
    pad_ref[:, :384] = zeros
    pad_ref[:, 384 + plane :] = zeros
    for p in range(planes):
        pad_ref[p * rows : (p + 1) * rows, 384 : 384 + plane] = x_ref[:, p * plane : (p + 1) * plane]

    def body(step, carry):
        start = pl.multiple_of(step * 256, 256)
        window = pad_ref[:, pl.ds(start, 1024)]
        acc = jnp.dot(window, w_ref[0], preferred_element_type=F32)
        acc += jnp.dot(window, w_ref[1], preferred_element_type=F32)
        acc += jnp.dot(window, w_ref[2], preferred_element_type=F32)
        mid = [window[p * rows : (p + 1) * rows, 384:640].astype(F32) for p in range(planes)]
        for p in range(planes):
            where = pl.multiple_of(p * plane + start, 256)
            value = acc[p * rows : (p + 1) * rows]
            value += (pot_ref[:, pl.ds(where, 256)] + 3.0 * HALF[0]) * mid[p]
            for q in range(planes):
                if q != p and abs(q - p) <= WIDTH:
                    value += HALF[abs(q - p)] * mid[q]
            out_ref[:, pl.ds(where, 256)] = value
        return carry

    lax.fori_loop(0, plane // 256, body, 0)


def hamilton_kernel(
    planes, block_ref, h0_ref, x_ref, left_ref, right_ref, sv_ref, proj_ref, h_ref, nd_ref
):
    rows, cells = x_ref.shape
    plane = cells // planes
    slots = proj_ref.shape[0]

    def halo(step, carry):
        for top in range(0, rows, 16):
            pick = slice(top, top + 16)
            before = []
            after = []
            for p in range(planes):
                where = pl.ds(pl.multiple_of(p * plane + step * BS, BS), BS)
                before.append(left_ref[pick, where].astype(F32))
                after.append(right_ref[pick, where].astype(F32))
            for p in range(planes):
                where = pl.ds(pl.multiple_of(p * plane + step * BS, BS), BS)
                value = h0_ref[pick, where]
                for j in range(p, planes):
                    value += HALF[planes + p - j] * before[j]
                for j in range(p + 1):
                    value += HALF[planes + j - p] * after[j]
                h_ref[pick, where] = value
        return carry

    lax.fori_loop(0, plane // BS, halo, 0)

    for s in range(slots):
        where = pl.ds(pl.multiple_of(block_ref[s] * BS, BS), BS)
        h_ref[:, where] += sv_ref[:, s : s + 1] * proj_ref[s : s + 1, :]

    def energy(step, carry):
        num, den = carry
        where = pl.ds(pl.multiple_of(step * BS, BS), BS)
        x = x_ref[:, where].astype(F32)
        return num + x * h_ref[:, where], den + x * x

    zero = jnp.zeros((rows, BS), F32)
    num, den = lax.fori_loop(0, cells // BS, energy, (zero, zero), unroll=4)
    lane = lax.broadcasted_iota(jnp.int32, (rows, BS), 1)
    num = jnp.sum(num, axis=1, keepdims=True)
    den = jnp.sum(den, axis=1, keepdims=True)
    nd_ref[...] = jnp.where(lane == 0, num, jnp.where(lane == 1, den, 0.0))


def residual_kernel(planes, h_ref, x_ref, e_ref, r_ref):
    parts, rows, width = r_ref.shape
    plane = x_ref.shape[1] // planes
    part = plane // parts
    energy = jnp.broadcast_to(e_ref[...], (rows, BS))
    for c in range(parts):
        for p in range(planes):
            for j in range(part // BS):
                src = p * plane + c * part + j * BS
                dst = p * part + j * BS
                value = h_ref[:, src : src + BS] - energy * x_ref[:, src : src + BS].astype(F32)
                r_ref[c, :, dst : dst + BS] = value.astype(BF16)


def ring(size):
    up = [(i, (i + 1) % size) for i in range(size)]
    return up, [(j, i) for i, j in up]


def spread(value, axis):
    size = lax.axis_size(axis)
    return lax.all_to_all(
        jnp.broadcast_to(value[None], (size,) + value.shape), axis, 0, 0, tiled=True
    )


def per_device(
    orbitals, potential, projectors, coupling, slot_block, slot_projector, slot_count, locked
):
    bands, planes, depth_z, width_y = orbitals.shape
    plane = depth_z * width_y
    cells = planes * plane
    domains = lax.axis_size(DOM)
    groups = lax.axis_size(BAND)
    n_x = lax.axis_size("x")
    core = lax.axis_index("core")
    here = lax.axis_index(DOM)
    slots = slot_block.shape[0]
    owned_count = coupling.shape[0]
    part = plane // groups
    n_locked = locked.shape[0]
    up, down = ring(domains)
    swap = [(0, 1), (1, 0)]

    flat = orbitals.reshape(bands, cells)
    pot = potential.reshape(1, cells)
    weights = jnp.asarray(plane_weights(width_y))

    active = jnp.arange(slots, dtype=jnp.int32) < slot_count[0]
    relative = (slot_projector // owned_count - here + domains) % domains
    section = jnp.where(relative == 0, 1, jnp.where(relative == 1, 2, 0))
    column = section * owned_count + slot_projector % owned_count
    onehot = (
        (column[:, None] == jnp.arange(BS, dtype=jnp.int32)[None, :]) & active[:, None]
    ).astype(F32)
    onehot_rows = jnp.pad(onehot, ((0, BS - slots), (0, 0)))
    locked_flat = locked.reshape(n_locked, planes * part)

    rows = bands // CHUNKS
    outs = []
    for k in range(CHUNKS):
        x = flat[k * rows : (k + 1) * rows]
        left = lax.ppermute(x, DOM, up)
        right = lax.ppermute(x, DOM, down)

        shares = pl.pallas_call(
            inner_kernel,
            out_shape=jax.ShapeDtypeStruct((rows, BS), F32),
            in_specs=[SMEM, VMEM, VMEM, VMEM],
            out_specs=VMEM,
            compiler_params=params(8),
            name="inner",
        )(slot_block, x, projectors, onehot_rows)
        n = owned_count
        to_down, mine, to_up = shares[:, :n], shares[:, n : 2 * n], shares[:, 2 * n : 3 * n]
        total = mine + lax.ppermute(to_up, DOM, up) + lax.ppermute(to_down, DOM, down)
        total = total * coupling[None]
        table = jnp.concatenate(
            [lax.ppermute(total, DOM, up), total, lax.ppermute(total, DOM, down)], axis=1
        )
        slot_value = jnp.dot(
            table, onehot[:, : 3 * n].T, precision=lax.Precision.HIGHEST
        )

        h0 = pl.pallas_call(
            functools.partial(local_kernel, planes),
            out_shape=jax.ShapeDtypeStruct((rows, cells), F32),
            in_specs=[VMEM, VMEM, VMEM],
            out_specs=VMEM,
            scratch_shapes=[pltpu.VMEM((planes * rows, plane + 768), BF16)],
            compiler_params=params(24),
            name="local",
        )(x, pot, weights)

        hamilton, sums = pl.pallas_call(
            functools.partial(hamilton_kernel, planes),
            out_shape=(
                jax.ShapeDtypeStruct((rows, cells), F32),
                jax.ShapeDtypeStruct((rows, BS), F32),
            ),
            in_specs=[SMEM] + [VMEM] * 6,
            out_specs=(VMEM, VMEM),
            compiler_params=params(24),
            name="hamilton",
        )(slot_block, h0, x, left, right, slot_value, projectors)
        sums = jnp.sum(spread(sums[:, :2].T[None], DOM), axis=0)
        sums = sums.reshape(2, rows)
        energy = (sums[0] / sums[1])[:, None]

        residual = pl.pallas_call(
            functools.partial(residual_kernel, planes),
            out_shape=jax.ShapeDtypeStruct((groups, rows, planes * part), BF16),
            in_specs=[VMEM] * 3,
            out_specs=VMEM,
            compiler_params=params(24),
            name="residual",
        )(hamilton, x, energy)
        moved = lax.all_to_all(residual, BAND, 0, 0, tiled=True)
        moved = moved.reshape(groups * rows, planes * part)

        partial = lax.dot_general(
            locked_flat, moved, (((1,), (1,)), ((), ())), preferred_element_type=F32
        )
        partial = partial.reshape(n_x, 2, n_locked // groups, groups * rows)
        kept = lax.dynamic_index_in_dim(partial, core, 1, keepdims=False)
        given = lax.dynamic_index_in_dim(partial, 1 - core, 1, keepdims=False)
        pair = kept + lax.ppermute(given, "core", swap)
        share = jnp.sum(lax.all_to_all(pair, "x", 0, 0, tiled=True), axis=0)
        share = share.reshape(domains, -1, groups * rows)
        margins = jnp.sum(lax.all_to_all(share, DOM, 0, 0, tiled=True), axis=0)

        coeffs = margins.astype(BF16)
        coeffs = spread(coeffs, DOM).reshape(n_locked // groups, groups * rows)
        coeffs = spread(coeffs, "x")
        coeffs = coeffs.reshape(n_x, n_locked // groups, groups * rows)
        other = lax.ppermute(coeffs, "core", swap)
        first = jnp.where(core == 0, coeffs, other)
        second = jnp.where(core == 0, other, coeffs)
        coeffs = jnp.stack([first, second], axis=1).reshape(n_locked, groups * rows)
        correction = lax.dot_general(
            coeffs, locked_flat, (((0,), (0,)), ((), ())), preferred_element_type=F32
        )
        orthogonal = (moved.astype(F32) - correction).astype(BF16)
        outs.append((orthogonal, margins))

    orthogonal = jnp.stack([o.reshape(groups, rows, planes, part) for o, _ in outs], axis=1)
    margins = jnp.stack([m.reshape(-1, groups, rows) for _, m in outs], axis=2)
    return (
        orthogonal.reshape(groups * bands, planes, part),
        margins.reshape(margins.shape[0], groups * bands),
    )


def solution(mesh):
    n_band, n_dom = mesh.devices.shape
    n_y = 4 if n_dom % 4 == 0 else 2
    fine = Mesh(
        mesh.devices.reshape(n_band // 2, 2, n_dom // n_y, n_y), ("x", "core", "z", "y")
    )
    in_specs = (
        P(BAND, DOM, None, None),
        P(DOM, None, None),
        P(DOM, None),
        P(DOM),
        P(DOM),
        P(DOM),
        P(DOM),
        P(None, DOM, BAND),
    )
    out_specs = (P(None, DOM, BAND), P(BAND + DOM, None))
    return jax.shard_map(
        per_device, mesh=fine, in_specs=in_specs, out_specs=out_specs, check_vma=False
    )
```

```python
import functools

import jax
import jax.numpy as jnp
import numpy as np
from jax import lax
from jax.experimental import pallas as pl
from jax.experimental.pallas import tpu as pltpu
from jax.sharding import Mesh
from jax.sharding import PartitionSpec as P

BS = 128

COEFFS = (
    -5369.0 / 1800.0,
    12.0 / 7.0,
    -15.0 / 56.0,
    10.0 / 189.0,
    -1.0 / 112.0,
    2.0 / 825.0,
    -1.0 / 5544.0,
)
HALF = tuple(-0.5 * c for c in COEFFS)
WIDTH = 6
DOM = ("z", "y")
BAND = ("x", "core")
F32 = jnp.float32
BF16 = jnp.bfloat16
VMEM = pl.BlockSpec(memory_space=pltpu.VMEM)
SMEM = pl.BlockSpec(memory_space=pltpu.SMEM)


def params(mib):
    return pltpu.CompilerParams(vmem_limit_bytes=mib * 1024 * 1024)


def cost(microseconds):
    return pl.CostEstimate(
        flops=0, transcendentals=0, bytes_accessed=int(microseconds * 3_000_000)
    )


@functools.lru_cache
def plane_weights(width_y):
    src = np.arange(1024)
    dst = np.arange(256)
    dz = np.abs((src // width_y - 2 * (384 // (2 * width_y)))[:, None] - (dst // width_y)[None])
    dy = np.abs((src % width_y)[:, None] - (dst % width_y)[None])
    dy = np.minimum(dy, width_y - dy)
    table = np.zeros(2048)
    table[1 : WIDTH + 1] = HALF[1:]
    full = np.where(dy == 0, table[dz], 0.0) + np.where(dz == 0, table[dy], 0.0)
    terms = []
    for _ in range(3):
        term = full.astype(np.float32).astype(BF16)
        terms.append(term)
        full = full - term.astype(np.float64)
    return np.stack(terms)


def inner_kernel(
    planes, block_ref, x_ref, proj_ref, onehot_ref, coupling_ref, share_ref, raw_ref, pack_ref
):
    rows = x_ref.shape[0]
    slots = proj_ref.shape[0]
    lane = lax.broadcasted_iota(jnp.int32, (rows, BS), 1)

    def body(s, acc):
        start = pl.multiple_of(block_ref[s] * BS, BS)
        cells = x_ref[:, pl.ds(start, BS)].astype(F32)
        total = jnp.sum(cells * proj_ref[pl.ds(s, 1), :], axis=1, keepdims=True)
        return jnp.where(lane == s, total, acc)

    acc = lax.fori_loop(0, slots, body, jnp.zeros((rows, BS), F32), unroll=8)
    raw_ref[...] = acc
    share_ref[:rows] = jnp.dot(
        acc, onehot_ref[...], precision=lax.Precision.HIGHEST, preferred_element_type=F32
    )
    share_ref[rows:] = coupling_ref[...]

    parts, _, width = pack_ref.shape
    plane = x_ref.shape[1] // planes
    part = plane // parts
    for c in range(parts):
        for p in range(planes):
            src = p * plane + c * part
            pack_ref[c, :, p * part : (p + 1) * part] = x_ref[:, src : src + part]


def local_kernel(planes, x_ref, pot_ref, w_ref, out_ref, den_ref, pad_ref):
    rows = x_ref.shape[0]
    plane = x_ref.shape[1] // planes
    zeros = jnp.zeros((planes * rows, 384), BF16)
    pad_ref[:, :384] = zeros
    pad_ref[:, 384 + plane :] = zeros
    for p in range(planes):
        pad_ref[p * rows : (p + 1) * rows, 384 : 384 + plane] = x_ref[:, p * plane : (p + 1) * plane]

    def body(step, den):
        start = pl.multiple_of(step * 256, 256)
        window = pad_ref[:, pl.ds(start, 1024)]
        acc = jnp.dot(window, w_ref[0], preferred_element_type=F32)
        acc += jnp.dot(window, w_ref[1], preferred_element_type=F32)
        acc += jnp.dot(window, w_ref[2], preferred_element_type=F32)
        mid = [window[p * rows : (p + 1) * rows, 384:640].astype(F32) for p in range(planes)]
        for p in range(planes):
            where = pl.multiple_of(p * plane + start, 256)
            value = acc[p * rows : (p + 1) * rows]
            value += (pot_ref[:, pl.ds(where, 256)] + 3.0 * HALF[0]) * mid[p]
            for q in range(planes):
                if q != p and abs(q - p) <= WIDTH:
                    value += HALF[abs(q - p)] * mid[q]
            out_ref[:, pl.ds(where, 256)] = value
            square = mid[p] * mid[p]
            den += square[:, :BS] + square[:, BS:]
        return den

    den_ref[...] = lax.fori_loop(0, plane // 256, body, jnp.zeros((rows, BS), F32))


def hamilton_kernel(
    planes,
    block_ref,
    group_ref,
    h0_ref,
    x_ref,
    left_ref,
    right_ref,
    proj_ref,
    onehot_ref,
    den_ref,
    raw_ref,
    mine_ref,
    left1_ref,
    left2_ref,
    right1_ref,
    right2_ref,
    r_ref,
    nd_ref,
    h_ref,
):
    rows, cells = x_ref.shape
    plane = cells // planes
    slots = proj_ref.shape[0]
    n = BS // 4

    def halo(step, carry):
        sums = []
        for top in range(0, rows, 16):
            pick = slice(top, top + 16)
            before = []
            after = []
            num = carry[top // 16]
            for p in range(planes):
                where = pl.ds(pl.multiple_of(p * plane + step * BS, BS), BS)
                before.append(left_ref[pick, where].astype(F32))
                after.append(right_ref[pick, where].astype(F32))
            for p in range(planes):
                where = pl.ds(pl.multiple_of(p * plane + step * BS, BS), BS)
                value = h0_ref[pick, where]
                for j in range(p, planes):
                    value += HALF[planes + p - j] * before[j]
                for j in range(p + 1):
                    value += HALF[planes + j - p] * after[j]
                h_ref[pick, where] = value
                num += value * x_ref[pick, where].astype(F32)
            sums.append(num)
        return tuple(sums)

    zero = jnp.zeros((16, BS), F32)
    num = lax.fori_loop(0, plane // BS, halo, (zero,) * (rows // 16))
    num = jnp.concatenate(num, axis=0)

    shape = mine_ref.shape
    at = lax.broadcasted_iota(jnp.int32, shape, 1)
    total = mine_ref[...]
    total += jnp.where(at < 2 * n, pltpu.roll(left1_ref[...], 3 * n, 1), 0.0)
    total += jnp.where(at < n, pltpu.roll(left2_ref[...], 2 * n, 1), 0.0)
    total += jnp.where((at >= n) & (at < 3 * n), pltpu.roll(right1_ref[...], n, 1), 0.0)
    total += jnp.where((at >= 2 * n) & (at < 3 * n), pltpu.roll(right2_ref[...], 2 * n, 1), 0.0)
    table = total[:rows] * total[rows : rows + 1]
    value = lax.dot_general(
        table,
        onehot_ref[...],
        (((1,), (1,)), ((), ())),
        precision=lax.Precision.HIGHEST,
        preferred_element_type=F32,
    )
    for s in range(slots):
        where = pl.ds(pl.multiple_of(block_ref[s] * BS, BS), BS)
        h_ref[:, where] += value[:, s : s + 1] * proj_ref[s : s + 1, :]

    num = jnp.sum(num + value * raw_ref[...], axis=1, keepdims=True)
    den = jnp.sum(den_ref[...], axis=1, keepdims=True)
    parts, _, width = r_ref.shape
    part = plane // parts
    energy = jnp.broadcast_to(jnp.where(den > 0.0, num / den, 0.0), (rows, BS))
    for c in range(parts):
        for p in range(planes):
            for j in range(part // BS):
                src = p * plane + c * part + j * BS
                dst = p * part + j * BS
                left = h_ref[:, src : src + BS] - energy * x_ref[:, src : src + BS].astype(F32)
                r_ref[c, :, dst : dst + BS] = left.astype(BF16)

    bands = nd_ref.shape[2]
    lane = lax.broadcasted_iota(jnp.int32, (rows, bands), 1)
    band = lax.broadcasted_iota(jnp.int32, (rows, bands), 0) + group_ref[0] * rows
    for i, column in enumerate((num, den)):
        line = jnp.sum(jnp.where(lane == band, column, 0.0), axis=0, keepdims=True)
        nd_ref[:, i : i + 1, :] = jnp.broadcast_to(line[None], (nd_ref.shape[0], 1, bands))


def margin_kernel(planes, fix, core_ref, locked_ref, *refs):
    if fix:
        h_ref, x_ref, sums_ref, out_ref, r_ref = refs

        @pl.when(pl.program_id(0) == 0)
        def _():
            bands = h_ref.shape[0]
            sums = jnp.sum(sums_ref[...], axis=0)
            own = jnp.where(sums[3:4] > 0.0, sums[2:3] / sums[3:4], 0.0)
            shift = sums[0:1] / sums[1:2] - own
            eye = lax.broadcasted_iota(jnp.int32, (bands, bands), 0) == lax.broadcasted_iota(
                jnp.int32, (bands, bands), 1
            )
            shift = jnp.sum(jnp.where(eye, shift, 0.0), axis=1, keepdims=True)
            for j in range(0, h_ref.shape[1], BS):
                where = slice(j, j + BS)
                value = h_ref[:, where].astype(F32) - shift * x_ref[:, where].astype(F32)
                r_ref[:, where] = value.astype(BF16)

    else:
        r_ref, out_ref = refs
    part = r_ref.shape[1] // planes
    acc = None
    for p in range(planes):
        term = lax.dot_general(
            locked_ref[p, 0, 0],
            r_ref[:, p * part : (p + 1) * part],
            (((1,), (1,)), ((), ())),
            preferred_element_type=F32,
        )
        acc = term if acc is None else acc + term
    out_ref[0] = acc


def clean_kernel(core_ref, locked_ref, mine_ref, other_ref, r_ref, out_ref, turned_ref):
    n_x = mine_ref.shape[0]
    core = core_ref[0]

    @pl.when(pl.program_id(0) == 0)
    def _():
        for i in range(n_x):
            turned_ref[0, i] = mine_ref[i].T
            turned_ref[1, i] = other_ref[i].T

    acc = None
    for side in range(2):
        for i in range(n_x):
            term = jnp.dot(
                turned_ref[side, i],
                locked_ref[0, i, jnp.where(side == 0, core, 1 - core)],
                preferred_element_type=F32,
            )
            acc = term if acc is None else acc + term
    out_ref[0] = (r_ref[...].astype(F32) - acc).astype(BF16)


def ring(size):
    up = [(i, (i + 1) % size) for i in range(size)]
    return up, [(j, i) for i, j in up]


def spread(value, axis):
    size = lax.axis_size(axis)
    return lax.all_to_all(
        jnp.broadcast_to(value[None], (size,) + value.shape), axis, 0, 0, tiled=True
    )


def per_device(
    orbitals, potential, projectors, coupling, slot_block, slot_projector, slot_count, locked
):
    rows, planes, depth_z, width_y = orbitals.shape
    plane = depth_z * width_y
    cells = planes * plane
    domains = lax.axis_size(DOM)
    groups = lax.axis_size(BAND)
    n_x = lax.axis_size("x")
    core = lax.axis_index("core").astype(jnp.int32)
    here = lax.axis_index(DOM)
    group = lax.axis_index(BAND).astype(jnp.int32)
    slots = slot_block.shape[0]
    n = coupling.shape[0]
    part = plane // groups
    width = planes * part
    n_locked = locked.shape[0]
    bands = groups * rows
    share_rows = n_locked // groups
    up, down = ring(domains)
    up2 = [(i, (i + 2) % domains) for i in range(domains)]
    down2 = [(j, i) for i, j in up2]
    swap = [(0, 1), (1, 0)]

    x = orbitals.reshape(rows, cells)
    left = lax.ppermute(x, DOM, up)
    right = lax.ppermute(x, DOM, down)

    pot = potential.reshape(1, cells)
    weights = jnp.asarray(plane_weights(width_y))
    active = jnp.arange(slots, dtype=jnp.int32) < slot_count[0]
    relative = (slot_projector // n - here + domains) % domains
    section = jnp.where(relative == 0, 1, jnp.where(relative == 1, 2, 0))
    column = section * n + slot_projector % n
    column = jnp.where(active, column, BS)
    column = jnp.pad(column, (0, BS - slots), constant_values=BS)
    onehot = (column[:, None] == jnp.arange(BS, dtype=jnp.int32)[None, :]).astype(F32)
    coupling_rows = jnp.pad(coupling[None], ((0, 7), (n, BS - 2 * n)))

    shares, raw, packed = pl.pallas_call(
        functools.partial(inner_kernel, planes),
        out_shape=(
            jax.ShapeDtypeStruct((rows + 8, BS), F32),
            jax.ShapeDtypeStruct((rows, BS), F32),
            jax.ShapeDtypeStruct((groups, rows, width), BF16),
        ),
        in_specs=[SMEM, VMEM, VMEM, VMEM, VMEM],
        out_specs=(VMEM, VMEM, VMEM),
        compiler_params=params(8),
        cost_estimate=cost(3),
        name="inner",
    )(slot_block, x, projectors, onehot, coupling_rows)
    left1 = lax.ppermute(shares, DOM, up)
    left2 = lax.ppermute(shares, DOM, up2)
    right1 = lax.ppermute(shares, DOM, down)
    right2 = lax.ppermute(shares, DOM, down2)
    x_moved = lax.all_to_all(packed, BAND, 0, 0, tiled=True).reshape(bands, width)

    h0, den = pl.pallas_call(
        functools.partial(local_kernel, planes),
        out_shape=(
            jax.ShapeDtypeStruct((rows, cells), F32),
            jax.ShapeDtypeStruct((rows, BS), F32),
        ),
        in_specs=[VMEM, VMEM, VMEM],
        out_specs=(VMEM, VMEM),
        scratch_shapes=[pltpu.VMEM((planes * rows, plane + 768), BF16)],
        compiler_params=params(24),
        cost_estimate=cost(7),
        name="local",
    )(x, pot, weights)

    sent, sums = pl.pallas_call(
        functools.partial(hamilton_kernel, planes),
        out_shape=(
            jax.ShapeDtypeStruct((groups, rows, width), BF16),
            jax.ShapeDtypeStruct((domains, 2, bands), F32),
        ),
        in_specs=[SMEM, SMEM] + [VMEM] * 13,
        out_specs=(VMEM, VMEM),
        scratch_shapes=[pltpu.VMEM((rows, cells), F32)],
        compiler_params=params(24),
        cost_estimate=cost(5),
        name="hamilton",
    )(
        slot_block,
        group.reshape(1),
        h0,
        x,
        left,
        right,
        projectors,
        onehot,
        den,
        raw,
        shares,
        left1,
        left2,
        right1,
        right2,
    )
    moved = lax.all_to_all(sent, BAND, 0, 0, tiled=True).reshape(bands, width)
    whole = jnp.sum(lax.all_to_all(sums, DOM, 0, 0, tiled=True), axis=0)
    sums = spread(jnp.concatenate([whole, sums[0]], axis=0), BAND)
    sums = sums.reshape(groups, 4, bands)

    by_plane = locked.transpose(1, 0, 2).reshape(planes, n_x, 2, share_rows, part)

    def margin_call(fix, side, *operands):
        full = pl.BlockSpec((bands, width), lambda i, c: (0, 0))
        out_spec = pl.BlockSpec((1, share_rows, bands), lambda i, c: (i, 0, 0))
        out_shape = jax.ShapeDtypeStruct((n_x, share_rows, bands), F32)
        extra = [pl.BlockSpec((groups, 4, bands), lambda i, c: (0, 0, 0))]
        return pl.pallas_call(
            functools.partial(margin_kernel, planes, fix),
            out_shape=(out_shape, jax.ShapeDtypeStruct((bands, width), BF16)) if fix else out_shape,
            grid_spec=pltpu.PrefetchScalarGridSpec(
                num_scalar_prefetch=1,
                grid=(n_x,),
                in_specs=[
                    pl.BlockSpec((planes, 1, 1, share_rows, part), lambda i, c: (0, i, c[0], 0, 0))
                ]
                + ([full, full] + extra if fix else [full]),
                out_specs=(out_spec, full) if fix else out_spec,
            ),
            compiler_params=params(24),
            cost_estimate=cost(3),
            name="margin",
        )(side.reshape(1), by_plane, *operands)

    given, residual = margin_call(True, 1 - core, moved, x_moved, sums)
    given = lax.ppermute(given, "core", swap)
    kept = margin_call(False, core, residual)
    pair = kept + given
    share = jnp.sum(lax.all_to_all(pair, "x", 0, 0, tiled=True), axis=0)
    share = share.reshape(domains, -1, bands)
    margins = jnp.sum(lax.all_to_all(share, DOM, 0, 0, tiled=True), axis=0)

    coeffs = spread(margins.astype(BF16), DOM).reshape(share_rows, bands)
    coeffs = spread(coeffs, "x").reshape(n_x, share_rows, bands)
    other = lax.ppermute(coeffs, "core", swap)
    whole_block = pl.BlockSpec((n_x, share_rows, bands), lambda p, c: (0, 0, 0))
    orthogonal = pl.pallas_call(
        clean_kernel,
        out_shape=jax.ShapeDtypeStruct((planes, bands, part), BF16),
        grid_spec=pltpu.PrefetchScalarGridSpec(
            num_scalar_prefetch=1,
            grid=(planes,),
            in_specs=[
                pl.BlockSpec((1, n_x, 2, share_rows, part), lambda p, c: (p, 0, 0, 0, 0)),
                whole_block,
                whole_block,
                pl.BlockSpec((bands, part), lambda p, c: (0, p)),
            ],
            out_specs=pl.BlockSpec((1, bands, part), lambda p, c: (p, 0, 0)),
            scratch_shapes=[pltpu.VMEM((2, n_x, bands, share_rows), BF16)],
        ),
        compiler_params=params(24),
        cost_estimate=cost(5),
        name="clean",
    )(core.reshape(1), by_plane, coeffs, other, residual)
    return orthogonal.transpose(1, 0, 2), margins


def solution(mesh):
    n_band, n_dom = mesh.devices.shape
    n_y = 4 if n_dom % 4 == 0 else 2
    fine = Mesh(
        mesh.devices.reshape(n_band // 2, 2, n_dom // n_y, n_y), ("x", "core", "z", "y")
    )
    in_specs = (
        P(BAND, DOM, None, None),
        P(DOM, None, None),
        P(DOM, None),
        P(DOM),
        P(DOM),
        P(DOM),
        P(DOM),
        P(None, DOM, BAND),
    )
    out_specs = (P(None, DOM, BAND), P(BAND + DOM, None))
    return jax.shard_map(
        per_device, mesh=fine, in_specs=in_specs, out_specs=out_specs, check_vma=False
    )
```

```python
import functools

import jax
import jax.numpy as jnp
import numpy as np
from jax import lax
from jax.experimental import pallas as pl
from jax.experimental.pallas import tpu as pltpu
from jax.sharding import Mesh
from jax.sharding import PartitionSpec as P

BS = 128

COEFFS = (
    -5369.0 / 1800.0,
    12.0 / 7.0,
    -15.0 / 56.0,
    10.0 / 189.0,
    -1.0 / 112.0,
    2.0 / 825.0,
    -1.0 / 5544.0,
)
HALF = tuple(-0.5 * c for c in COEFFS)
WIDTH = 6
DOM = ("z", "y")
BAND = ("x", "core")
EACH = ("x", "z", "y")
F32 = jnp.float32
BF16 = jnp.bfloat16
VMEM = pl.BlockSpec(memory_space=pltpu.VMEM)
SMEM = pl.BlockSpec(memory_space=pltpu.SMEM)


def params(mib):
    return pltpu.CompilerParams(vmem_limit_bytes=mib * 1024 * 1024)


def cost(microseconds):
    return pl.CostEstimate(
        flops=0, transcendentals=0, bytes_accessed=int(microseconds * 3_000_000)
    )


@functools.lru_cache
def plane_weights(width_y):
    src = np.arange(1024)
    dst = np.arange(256)
    dz = np.abs((src // width_y - 2 * (384 // (2 * width_y)))[:, None] - (dst // width_y)[None])
    dy = np.abs((src % width_y)[:, None] - (dst % width_y)[None])
    dy = np.minimum(dy, width_y - dy)
    table = np.zeros(2048)
    table[1 : WIDTH + 1] = HALF[1:]
    full = np.where(dy == 0, table[dz], 0.0) + np.where(dz == 0, table[dy], 0.0)
    terms = []
    for _ in range(3):
        term = full.astype(np.float32).astype(BF16)
        terms.append(term)
        full = full - term.astype(np.float64)
    return np.stack(terms)


def inner_kernel(block_ref, x_ref, proj_ref, onehot_ref, share_ref):
    rows = x_ref.shape[0]
    slots = proj_ref.shape[0]
    lane = lax.broadcasted_iota(jnp.int32, (rows, BS), 1)

    def body(s, acc):
        start = pl.multiple_of(block_ref[s] * BS, BS)
        cells = x_ref[:, pl.ds(start, BS)].astype(F32)
        total = jnp.sum(cells * proj_ref[pl.ds(s, 1), :], axis=1, keepdims=True)
        return jnp.where(lane == s, total, acc)

    acc = lax.fori_loop(0, slots, body, jnp.zeros((rows, BS), F32), unroll=8)
    share_ref[...] = jnp.dot(
        acc, onehot_ref[...], precision=lax.Precision.HIGHEST, preferred_element_type=F32
    )


def local_kernel(planes, x_ref, pot_ref, w_ref, out_ref, den_ref, pad_ref):
    rows = x_ref.shape[0]
    plane = x_ref.shape[1] // planes
    zeros = jnp.zeros((planes * rows, 384), BF16)
    pad_ref[:, :384] = zeros
    pad_ref[:, 384 + plane :] = zeros
    for p in range(planes):
        pad_ref[p * rows : (p + 1) * rows, 384 : 384 + plane] = x_ref[:, p * plane : (p + 1) * plane]

    def body(step, den):
        start = pl.multiple_of(step * 256, 256)
        window = pad_ref[:, pl.ds(start, 1024)]
        acc = jnp.dot(window, w_ref[0], preferred_element_type=F32)
        acc += jnp.dot(window, w_ref[1], preferred_element_type=F32)
        acc += jnp.dot(window, w_ref[2], preferred_element_type=F32)
        mid = [window[p * rows : (p + 1) * rows, 384:640].astype(F32) for p in range(planes)]
        for p in range(planes):
            where = pl.multiple_of(p * plane + start, 256)
            value = acc[p * rows : (p + 1) * rows]
            value += (pot_ref[:, pl.ds(where, 256)] + 3.0 * HALF[0]) * mid[p]
            for q in range(planes):
                if q != p and abs(q - p) <= WIDTH:
                    value += HALF[abs(q - p)] * mid[q]
            out_ref[:, pl.ds(where, 256)] = value
            square = mid[p] * mid[p]
            den += square[:, :BS] + square[:, BS:]
        return den

    den_ref[...] = lax.fori_loop(0, plane // 256, body, jnp.zeros((rows, BS), F32))


def hamilton_kernel(
    planes,
    h0_ref,
    x_ref,
    left_ref,
    right_ref,
    den_ref,
    mine_ref,
    below_ref,
    above_ref,
    coupling_ref,
    h_ref,
    table_ref,
    nd_ref,
):
    rows, cells = x_ref.shape
    plane = cells // planes
    n = BS // 4

    def halo(step, carry):
        sums = []
        for top in range(0, rows, 16):
            pick = slice(top, top + 16)
            before = []
            after = []
            num = carry[top // 16]
            for p in range(planes):
                where = pl.ds(pl.multiple_of(p * plane + step * BS, BS), BS)
                before.append(left_ref[pick, where].astype(F32))
                after.append(right_ref[pick, where].astype(F32))
            for p in range(planes):
                where = pl.ds(pl.multiple_of(p * plane + step * BS, BS), BS)
                value = h0_ref[pick, where]
                for j in range(p, planes):
                    value += HALF[planes + p - j] * before[j]
                for j in range(p + 1):
                    value += HALF[planes + j - p] * after[j]
                h_ref[pick, where] = value
                num += value * x_ref[pick, where].astype(F32)
            sums.append(num)
        return tuple(sums)

    zero = jnp.zeros((16, BS), F32)
    num = lax.fori_loop(0, plane // BS, halo, (zero,) * (rows // 16))
    num = jnp.concatenate(num, axis=0)

    lane = lax.broadcasted_iota(jnp.int32, (rows, BS), 1)
    row = lax.broadcasted_iota(jnp.int32, (rows, BS), 0)
    total = mine_ref[...]
    total += pltpu.roll(below_ref[...], 3 * n, 1)
    total += pltpu.roll(above_ref[...], n, 1)
    table = total * coupling_ref[...]
    table_ref[...] = table
    num = jnp.sum(num + table * total, axis=1, keepdims=True)
    den = jnp.sum(den_ref[...], axis=1, keepdims=True)
    line = jnp.where(lane == row, num, 0.0) + jnp.where(lane == row + rows, den, 0.0)
    line = jnp.sum(line, axis=0, keepdims=True)
    nd_ref[...] = jnp.broadcast_to(line[None], nd_ref.shape)


def residual_kernel(
    planes,
    block_ref,
    h_ref,
    x_ref,
    nd_ref,
    proj_ref,
    onehot_ref,
    mine_ref,
    below_ref,
    above_ref,
    r_ref,
    full_ref,
):
    rows, cells = x_ref.shape
    plane = cells // planes
    slots = proj_ref.shape[0]
    n = BS // 4
    table = mine_ref[...] + pltpu.roll(below_ref[...], 3 * n, 1)
    table += pltpu.roll(above_ref[...], n, 1)
    value = lax.dot_general(
        table,
        onehot_ref[...],
        (((1,), (1,)), ((), ())),
        precision=lax.Precision.HIGHEST,
        preferred_element_type=F32,
    )
    lane = lax.broadcasted_iota(jnp.int32, (rows, BS), 1)
    row = lax.broadcasted_iota(jnp.int32, (rows, BS), 0)
    sums = jnp.sum(nd_ref[...], axis=0)
    num = jnp.sum(jnp.where(lane == row, sums, 0.0), axis=1, keepdims=True)
    den = jnp.sum(jnp.where(lane == row + rows, sums, 0.0), axis=1, keepdims=True)
    energy = jnp.broadcast_to(num / den, (rows, BS))
    for at in range(0, cells, BS):
        where = slice(at, at + BS)
        full_ref[:, where] = h_ref[:, where] - energy * x_ref[:, where].astype(F32)

    for s in range(slots):
        where = pl.ds(pl.multiple_of(block_ref[s] * BS, BS), BS)
        full_ref[:, where] += value[:, s : s + 1] * proj_ref[s : s + 1, :]

    parts = r_ref.shape[0]
    part = plane // parts
    for c in range(parts):
        for p in range(planes):
            src = p * plane + c * part
            r_ref[c, :, p * part : (p + 1) * part] = full_ref[:, src : src + part].astype(BF16)


def margin_kernel(planes, core_ref, locked_ref, r_ref, out_ref):
    part = r_ref.shape[1] // planes
    acc = None
    for p in range(planes):
        term = lax.dot_general(
            locked_ref[p, 0, 0],
            r_ref[:, p * part : (p + 1) * part],
            (((1,), (1,)), ((), ())),
            preferred_element_type=F32,
        )
        acc = term if acc is None else acc + term
    out_ref[0] = acc


def clean_kernel(core_ref, locked_ref, mine_ref, other_ref, r_ref, out_ref, turned_ref):
    n_x = mine_ref.shape[0]
    core = core_ref[0]

    @pl.when(pl.program_id(0) == 0)
    def _():
        for i in range(n_x):
            turned_ref[0, i] = mine_ref[i].T
            turned_ref[1, i] = other_ref[i].T

    acc = None
    for side in range(2):
        for i in range(n_x):
            term = jnp.dot(
                turned_ref[side, i],
                locked_ref[0, i, jnp.where(side == 0, core, 1 - core)],
                preferred_element_type=F32,
            )
            acc = term if acc is None else acc + term
    out_ref[0] = (r_ref[...].astype(F32) - acc).astype(BF16)


def ring(size):
    up = [(i, (i + 1) % size) for i in range(size)]
    return up, [(j, i) for i, j in up]


def spread(value, axis):
    size = lax.axis_size(axis)
    return lax.all_to_all(
        jnp.broadcast_to(value[None], (size,) + value.shape), axis, 0, 0, tiled=True
    )


def per_device(
    orbitals, potential, projectors, coupling, slot_block, slot_projector, slot_count, locked
):
    rows, planes, depth_z, width_y = orbitals.shape
    plane = depth_z * width_y
    cells = planes * plane
    domains = lax.axis_size(DOM)
    groups = lax.axis_size(BAND)
    n_x = lax.axis_size("x")
    core = lax.axis_index("core").astype(jnp.int32)
    here = lax.axis_index(DOM)
    slots = slot_block.shape[0]
    n = coupling.shape[0]
    part = plane // groups
    width = planes * part
    n_locked = locked.shape[0]
    bands = groups * rows
    share_rows = n_locked // groups
    up, down = ring(domains)
    swap = [(0, 1), (1, 0)]

    x = orbitals.reshape(rows, cells)
    left = lax.ppermute(x, DOM, up)
    right = lax.ppermute(x, DOM, down)

    pot = potential.reshape(1, cells)
    weights = jnp.asarray(plane_weights(width_y))
    active = jnp.arange(slots, dtype=jnp.int32) < slot_count[0]
    relative = (slot_projector // n - here + domains) % domains
    section = jnp.where(relative == 0, 1, jnp.where(relative == 1, 2, 0))
    column = section * n + slot_projector % n
    column = jnp.where(active, column, BS)
    column = jnp.pad(column, (0, BS - slots), constant_values=BS)
    onehot = (column[:, None] == jnp.arange(BS, dtype=jnp.int32)[None, :]).astype(F32)
    coupling_row = jnp.pad(coupling[None], ((0, 0), (n, BS - 2 * n)))

    shares = pl.pallas_call(
        inner_kernel,
        out_shape=jax.ShapeDtypeStruct((rows, BS), F32),
        in_specs=[SMEM, VMEM, VMEM, VMEM],
        out_specs=VMEM,
        compiler_params=params(8),
        cost_estimate=cost(2),
        name="inner",
    )(slot_block, x, projectors, onehot)
    below = lax.ppermute(shares, DOM, up)
    above = lax.ppermute(shares, DOM, down)

    h0, den = pl.pallas_call(
        functools.partial(local_kernel, planes),
        out_shape=(
            jax.ShapeDtypeStruct((rows, cells), F32),
            jax.ShapeDtypeStruct((rows, BS), F32),
        ),
        in_specs=[VMEM, VMEM, VMEM],
        out_specs=(VMEM, VMEM),
        scratch_shapes=[pltpu.VMEM((planes * rows, plane + 768), BF16)],
        compiler_params=params(24),
        cost_estimate=cost(7),
        name="local",
    )(x, pot, weights)

    hamilton, table, sums = pl.pallas_call(
        functools.partial(hamilton_kernel, planes),
        out_shape=(
            jax.ShapeDtypeStruct((rows, cells), F32),
            jax.ShapeDtypeStruct((rows, BS), F32),
            jax.ShapeDtypeStruct((domains, 1, BS), F32),
        ),
        in_specs=[VMEM] * 9,
        out_specs=(VMEM, VMEM, VMEM),
        compiler_params=params(24),
        cost_estimate=cost(5),
        name="hamilton",
    )(h0, x, left, right, den, shares, below, above, coupling_row)
    table_below = lax.ppermute(table, DOM, up)
    table_above = lax.ppermute(table, DOM, down)
    sums = lax.all_to_all(sums, DOM, 0, 0, tiled=True)

    residual = pl.pallas_call(
        functools.partial(residual_kernel, planes),
        out_shape=jax.ShapeDtypeStruct((groups, rows, width), BF16),
        in_specs=[SMEM] + [VMEM] * 8,
        out_specs=VMEM,
        scratch_shapes=[pltpu.VMEM((rows, cells), F32)],
        compiler_params=params(24),
        cost_estimate=cost(2),
        name="residual",
    )(
        slot_block,
        hamilton,
        x,
        sums,
        projectors,
        onehot,
        table,
        table_below,
        table_above,
    )
    residual = lax.all_to_all(residual, BAND, 0, 0, tiled=True).reshape(bands, width)

    by_plane = locked.transpose(1, 0, 2).reshape(planes, n_x, 2, share_rows, part)
    by_plane = pltpu.with_memory_space_constraint(by_plane, pltpu.HBM)

    def margin_call(side):
        return pl.pallas_call(
            functools.partial(margin_kernel, planes),
            out_shape=jax.ShapeDtypeStruct((n_x, share_rows, bands), F32),
            grid_spec=pltpu.PrefetchScalarGridSpec(
                num_scalar_prefetch=1,
                grid=(n_x,),
                in_specs=[
                    pl.BlockSpec((planes, 1, 1, share_rows, part), lambda i, c: (0, i, c[0], 0, 0)),
                    pl.BlockSpec((bands, width), lambda i, c: (0, 0)),
                ],
                out_specs=pl.BlockSpec((1, share_rows, bands), lambda i, c: (i, 0, 0)),
            ),
            compiler_params=params(24),
            cost_estimate=cost(3),
            name="margin",
        )(side.reshape(1), by_plane, residual)

    given = lax.ppermute(margin_call(1 - core), "core", swap)
    pair = margin_call(core) + given
    share = pair.reshape(n_x * domains, -1, bands)
    margins = jnp.sum(lax.all_to_all(share, EACH, 0, 0, tiled=True), axis=0)

    coeffs = spread(margins.astype(BF16), EACH).reshape(n_x, share_rows, bands)
    other = lax.ppermute(coeffs, "core", swap)
    whole_block = pl.BlockSpec((n_x, share_rows, bands), lambda p, c: (0, 0, 0))
    orthogonal = pl.pallas_call(
        clean_kernel,
        out_shape=jax.ShapeDtypeStruct((planes, bands, part), BF16),
        grid_spec=pltpu.PrefetchScalarGridSpec(
            num_scalar_prefetch=1,
            grid=(planes,),
            in_specs=[
                pl.BlockSpec((1, n_x, 2, share_rows, part), lambda p, c: (p, 0, 0, 0, 0)),
                whole_block,
                whole_block,
                pl.BlockSpec((bands, part), lambda p, c: (0, p)),
            ],
            out_specs=pl.BlockSpec((1, bands, part), lambda p, c: (p, 0, 0)),
            scratch_shapes=[pltpu.VMEM((2, n_x, bands, share_rows), BF16)],
        ),
        compiler_params=params(24),
        cost_estimate=cost(5),
        name="clean",
    )(core.reshape(1), by_plane, coeffs, other, residual)
    return orthogonal.transpose(1, 0, 2), margins


def solution(mesh):
    n_band, n_dom = mesh.devices.shape
    n_y = 4 if n_dom % 4 == 0 else 2
    fine = Mesh(
        mesh.devices.reshape(n_band // 2, 2, n_dom // n_y, n_y), ("x", "core", "z", "y")
    )
    in_specs = (
        P(BAND, DOM, None, None),
        P(DOM, None, None),
        P(DOM, None),
        P(DOM),
        P(DOM),
        P(DOM),
        P(DOM),
        P(None, DOM, BAND),
    )
    out_specs = (P(None, DOM, BAND), P(BAND + DOM, None))
    return jax.shard_map(
        per_device, mesh=fine, in_specs=in_specs, out_specs=out_specs, check_vma=False
    )
```

```python
import functools

import jax
import jax.numpy as jnp
import numpy as np
from jax import lax
from jax.experimental import pallas as pl
from jax.experimental.pallas import tpu as pltpu
from jax.sharding import Mesh
from jax.sharding import PartitionSpec as P

BS = 128

COEFFS = (
    -5369.0 / 1800.0,
    12.0 / 7.0,
    -15.0 / 56.0,
    10.0 / 189.0,
    -1.0 / 112.0,
    2.0 / 825.0,
    -1.0 / 5544.0,
)
HALF = tuple(-0.5 * c for c in COEFFS)
WIDTH = 6
DOM = ("z", "y")
BAND = ("x", "core")
SHORT = ("x", "y")
F32 = jnp.float32
BF16 = jnp.bfloat16
VMEM = pl.BlockSpec(memory_space=pltpu.VMEM)
SMEM = pl.BlockSpec(memory_space=pltpu.SMEM)
ANY = pl.BlockSpec(memory_space=pl.ANY)


def params(mib):
    return pltpu.CompilerParams(vmem_limit_bytes=mib * 1024 * 1024)


def cost(microseconds):
    return pl.CostEstimate(
        flops=0, transcendentals=0, bytes_accessed=int(microseconds * 3_000_000)
    )


@functools.lru_cache
def plane_weights(width_y):
    src = np.arange(1024)
    dst = np.arange(256)
    dz = np.abs((src // width_y - 2 * (384 // (2 * width_y)))[:, None] - (dst // width_y)[None])
    dy = np.abs((src % width_y)[:, None] - (dst % width_y)[None])
    dy = np.minimum(dy, width_y - dy)
    table = np.zeros(2048)
    table[1 : WIDTH + 1] = HALF[1:]
    full = np.where(dy == 0, table[dz], 0.0) + np.where(dz == 0, table[dy], 0.0)
    terms = []
    for _ in range(3):
        term = full.astype(np.float32).astype(BF16)
        terms.append(term)
        full = full - term.astype(np.float64)
    return np.stack(terms)


def inner_kernel(block_ref, x_ref, proj_ref, onehot_ref, share_ref):
    rows = x_ref.shape[0]
    slots = proj_ref.shape[0]
    lane = lax.broadcasted_iota(jnp.int32, (rows, BS), 1)

    def body(s, acc):
        start = pl.multiple_of(block_ref[s] * BS, BS)
        cells = x_ref[:, pl.ds(start, BS)].astype(F32)
        total = jnp.sum(cells * proj_ref[pl.ds(s, 1), :], axis=1, keepdims=True)
        return jnp.where(lane == s, total, acc)

    acc = lax.fori_loop(0, slots, body, jnp.zeros((rows, BS), F32), unroll=8)
    share_ref[...] = jnp.dot(
        acc, onehot_ref[...], precision=lax.Precision.HIGHEST, preferred_element_type=F32
    )


def local_kernel(planes, x_ref, pot_ref, w_ref, out_ref, den_ref, pad_ref):
    rows = x_ref.shape[0]
    plane = x_ref.shape[1] // planes
    zeros = jnp.zeros((planes * rows, 384), BF16)
    pad_ref[:, :384] = zeros
    pad_ref[:, 384 + plane :] = zeros
    for p in range(planes):
        pad_ref[p * rows : (p + 1) * rows, 384 : 384 + plane] = x_ref[:, p * plane : (p + 1) * plane]

    def body(step, den):
        start = pl.multiple_of(step * 256, 256)
        window = pad_ref[:, pl.ds(start, 1024)]
        acc = jnp.dot(window, w_ref[0], preferred_element_type=F32)
        acc += jnp.dot(window, w_ref[1], preferred_element_type=F32)
        acc += jnp.dot(window, w_ref[2], preferred_element_type=F32)
        mid = [window[p * rows : (p + 1) * rows, 384:640].astype(F32) for p in range(planes)]
        for p in range(planes):
            where = pl.multiple_of(p * plane + start, 256)
            value = acc[p * rows : (p + 1) * rows]
            value += (pot_ref[:, pl.ds(where, 256)] + 3.0 * HALF[0]) * mid[p]
            for q in range(planes):
                if q != p and abs(q - p) <= WIDTH:
                    value += HALF[abs(q - p)] * mid[q]
            out_ref[:, pl.ds(where, 256)] = value
            square = mid[p] * mid[p]
            den += square[:, :BS] + square[:, BS:]
        return den

    den_ref[...] = lax.fori_loop(0, plane // 256, body, jnp.zeros((rows, BS), F32))


def hamilton_kernel(
    planes,
    h0_ref,
    x_ref,
    left_ref,
    right_ref,
    den_ref,
    mine_ref,
    coupling_ref,
    below_hbm,
    above_hbm,
    h_ref,
    pay_ref,
    below_ref,
    above_ref,
    sems,
):
    late = [
        pltpu.make_async_copy(below_hbm, below_ref, sems.at[0]),
        pltpu.make_async_copy(above_hbm, above_ref, sems.at[1]),
    ]
    for copy in late:
        copy.start()
    rows, cells = x_ref.shape
    plane = cells // planes
    n = BS // 4

    def halo(step, carry):
        sums = []
        for top in range(0, rows, 16):
            pick = slice(top, top + 16)
            before = []
            after = []
            num = carry[top // 16]
            for p in range(planes):
                where = pl.ds(pl.multiple_of(p * plane + step * BS, BS), BS)
                before.append(left_ref[pick, where].astype(F32))
                after.append(right_ref[pick, where].astype(F32))
            for p in range(planes):
                where = pl.ds(pl.multiple_of(p * plane + step * BS, BS), BS)
                value = h0_ref[pick, where]
                for j in range(p, planes):
                    value += HALF[planes + p - j] * before[j]
                for j in range(p + 1):
                    value += HALF[planes + j - p] * after[j]
                h_ref[pick, where] = value
                num += value * x_ref[pick, where].astype(F32)
            sums.append(num)
        return tuple(sums)

    zero = jnp.zeros((16, BS), F32)
    num = lax.fori_loop(0, plane // BS, halo, (zero,) * (rows // 16))
    num = jnp.concatenate(num, axis=0)

    for copy in late:
        copy.wait()
    lane = lax.broadcasted_iota(jnp.int32, (rows, BS), 1)
    row = lax.broadcasted_iota(jnp.int32, (rows, BS), 0)
    total = mine_ref[...]
    total += pltpu.roll(below_ref[...], 3 * n, 1)
    total += pltpu.roll(above_ref[...], n, 1)
    table = total * coupling_ref[...]
    num = jnp.sum(num + table * total, axis=1, keepdims=True)
    den = jnp.sum(den_ref[...], axis=1, keepdims=True)
    line = jnp.where(lane == row, num, 0.0) + jnp.where(lane == row + rows, den, 0.0)
    line = jnp.sum(line, axis=0, keepdims=True)

    short = rows // 4
    packed = None
    for g in range(4):
        piece = table[g * short : (g + 1) * short]
        piece = piece if g == 1 else pltpu.roll(piece, (g + 3) % 4 * n, 1)
        packed = piece if packed is None else packed + piece
    for r in range(short):
        pay_ref[:, r] = jnp.broadcast_to(packed[r : r + 1][None], (pay_ref.shape[0], 1, BS))
    pay_ref[:, short] = jnp.broadcast_to(line[None], (pay_ref.shape[0], 1, BS))


def residual_kernel(
    planes,
    block_ref,
    near_ref,
    h_ref,
    x_ref,
    pay_ref,
    proj_hbm,
    onehot_hbm,
    r_ref,
    full_ref,
    proj_ref,
    onehot_ref,
    sems,
):
    late = [
        pltpu.make_async_copy(proj_hbm, proj_ref, sems.at[0]),
        pltpu.make_async_copy(onehot_hbm, onehot_ref, sems.at[1]),
    ]
    for copy in late:
        copy.start()
    rows, cells = x_ref.shape
    plane = cells // planes
    slots = proj_ref.shape[0]
    n = BS // 4
    short = rows // 4
    lane = lax.broadcasted_iota(jnp.int32, (rows, BS), 1)
    row = lax.broadcasted_iota(jnp.int32, (rows, BS), 0)
    sums = jnp.sum(pay_ref[:, short], axis=0)
    num = jnp.sum(jnp.where(lane == row, sums, 0.0), axis=1, keepdims=True)
    den = jnp.sum(jnp.where(lane == row + rows, sums, 0.0), axis=1, keepdims=True)
    energy = jnp.broadcast_to(num / den, (rows, BS))
    for at in range(0, cells, BS):
        where = slice(at, at + BS)
        full_ref[:, where] = h_ref[:, where] - energy * x_ref[:, where].astype(F32)

    table = jnp.zeros((rows, BS), F32)
    for section in range(3):
        packed = jnp.concatenate(
            [pay_ref[near_ref[section], r] for r in range(short)], axis=0
        )
        pieces = [
            packed if g == section else pltpu.roll(packed, (section - g) % 4 * n, 1)
            for g in range(4)
        ]
        whole = jnp.concatenate(pieces, axis=0)
        table += jnp.where((lane >= section * n) & (lane < (section + 1) * n), whole, 0.0)
    for copy in late:
        copy.wait()
    value = lax.dot_general(
        table,
        onehot_ref[...],
        (((1,), (1,)), ((), ())),
        precision=lax.Precision.HIGHEST,
        preferred_element_type=F32,
    )
    for s in range(slots):
        where = pl.ds(pl.multiple_of(block_ref[s] * BS, BS), BS)
        full_ref[:, where] += value[:, s : s + 1] * proj_ref[s : s + 1, :]

    parts = r_ref.shape[0]
    part = plane // parts
    for c in range(parts):
        for p in range(planes):
            src = p * plane + c * part
            r_ref[c, :, p * part : (p + 1) * part] = full_ref[:, src : src + part].astype(BF16)


def margin_kernel(planes, core_ref, *refs):
    *locked_refs, r_ref, out_ref = refs
    part = r_ref.shape[1] // planes
    acc = None
    for p in range(planes):
        term = lax.dot_general(
            locked_refs[p][0, 0, 0],
            r_ref[:, p * part : (p + 1) * part],
            (((1,), (1,)), ((), ())),
            preferred_element_type=F32,
        )
        acc = term if acc is None else acc + term
    out_ref[0] = acc


def clean_kernel(core_ref, *refs):
    *locked_refs, mine_ref, other_ref, r_ref, out_ref, turned_ref = refs
    n_x = mine_ref.shape[0]
    core = core_ref[0]

    @pl.when(pl.program_id(0) == 0)
    def _():
        for i in range(n_x):
            turned_ref[0, i] = mine_ref[i].T
            turned_ref[1, i] = other_ref[i].T

    acc = None
    for side in range(2):
        for i in range(n_x):
            term = jnp.dot(
                turned_ref[side, i],
                locked_refs[i][0, 0, jnp.where(side == 0, core, 1 - core)],
                preferred_element_type=F32,
            )
            acc = term if acc is None else acc + term
    out_ref[0] = (r_ref[...].astype(F32) - acc).astype(BF16)


def ring(size):
    up = [(i, (i + 1) % size) for i in range(size)]
    return up, [(j, i) for i, j in up]


def spread(value, axis):
    size = lax.axis_size(axis)
    return lax.all_to_all(
        jnp.broadcast_to(value[None], (size,) + value.shape), axis, 0, 0, tiled=True
    )


def per_device(
    orbitals, potential, projectors, coupling, slot_block, slot_projector, slot_count, locked
):
    rows, planes, depth_z, width_y = orbitals.shape
    plane = depth_z * width_y
    cells = planes * plane
    domains = lax.axis_size(DOM)
    groups = lax.axis_size(BAND)
    n_x = lax.axis_size("x")
    n_z = lax.axis_size("z")
    n_y = lax.axis_size("y")
    core = lax.axis_index("core").astype(jnp.int32)
    here = lax.axis_index(DOM)
    slots = slot_block.shape[0]
    n = coupling.shape[0]
    part = plane // groups
    width = planes * part
    n_locked = locked.shape[0]
    bands = groups * rows
    share_rows = n_locked // groups
    up, down = ring(domains)
    swap = [(0, 1), (1, 0)]

    x = orbitals.reshape(rows, cells)
    left = lax.ppermute(x, DOM, up)
    right = lax.ppermute(x, DOM, down)

    pot = potential.reshape(1, cells)
    weights = jnp.asarray(plane_weights(width_y))
    active = jnp.arange(slots, dtype=jnp.int32) < slot_count[0]
    relative = (slot_projector // n - here + domains) % domains
    section = jnp.where(relative == 0, 1, jnp.where(relative == 1, 2, 0))
    column = section * n + slot_projector % n
    column = jnp.where(active, column, BS)
    column = jnp.pad(column, (0, BS - slots), constant_values=BS)
    onehot = (column[:, None] == jnp.arange(BS, dtype=jnp.int32)[None, :]).astype(F32)
    coupling_row = jnp.pad(coupling[None], ((0, 0), (n, BS - 2 * n)))

    shares = pl.pallas_call(
        inner_kernel,
        out_shape=jax.ShapeDtypeStruct((rows, BS), F32),
        in_specs=[SMEM, VMEM, VMEM, VMEM],
        out_specs=VMEM,
        compiler_params=params(8),
        cost_estimate=cost(2),
        name="inner",
    )(slot_block, x, projectors, onehot)
    below = lax.ppermute(shares, DOM, up)
    above = lax.ppermute(shares, DOM, down)

    h0, den = pl.pallas_call(
        functools.partial(local_kernel, planes),
        out_shape=(
            jax.ShapeDtypeStruct((rows, cells), F32),
            jax.ShapeDtypeStruct((rows, BS), F32),
        ),
        in_specs=[VMEM, VMEM, VMEM],
        out_specs=(VMEM, VMEM),
        scratch_shapes=[pltpu.VMEM((planes * rows, plane + 768), BF16)],
        compiler_params=params(24),
        cost_estimate=cost(7),
        name="local",
    )(x, pot, weights)

    hamilton, pay = pl.pallas_call(
        functools.partial(hamilton_kernel, planes),
        out_shape=(
            jax.ShapeDtypeStruct((rows, cells), F32),
            jax.ShapeDtypeStruct((domains, rows // 4 + 1, 1, BS), F32),
        ),
        in_specs=[VMEM] * 7 + [ANY] * 2,
        out_specs=(VMEM, VMEM),
        scratch_shapes=[
            pltpu.VMEM((rows, BS), F32),
            pltpu.VMEM((rows, BS), F32),
            pltpu.SemaphoreType.DMA((2,)),
        ],
        compiler_params=params(24),
        cost_estimate=cost(5),
        name="hamilton",
    )(h0, x, left, right, den, shares, coupling_row, below, above)
    pay = lax.all_to_all(pay, DOM, 0, 0, tiled=True)
    near = (here + domains + jnp.arange(-1, 2, dtype=jnp.int32)) % domains

    residual = pl.pallas_call(
        functools.partial(residual_kernel, planes),
        out_shape=jax.ShapeDtypeStruct((groups, rows, width), BF16),
        in_specs=[SMEM, SMEM] + [VMEM] * 3 + [ANY] * 2,
        out_specs=VMEM,
        scratch_shapes=[
            pltpu.VMEM((rows, cells), F32),
            pltpu.VMEM((slots, BS), F32),
            pltpu.VMEM((BS, BS), F32),
            pltpu.SemaphoreType.DMA((2,)),
        ],
        compiler_params=params(24),
        cost_estimate=cost(2),
        name="residual",
    )(slot_block, near.astype(jnp.int32), hamilton, x, pay, projectors, onehot)
    residual = lax.all_to_all(residual, BAND, 0, 0, tiled=True).reshape(bands, width)

    by_plane = locked.transpose(1, 0, 2).reshape(planes, n_x, 2, share_rows, part)
    by_plane = pltpu.with_memory_space_constraint(by_plane, pltpu.HBM)

    def margin_call(side):
        return pl.pallas_call(
            functools.partial(margin_kernel, planes),
            out_shape=jax.ShapeDtypeStruct((n_x, share_rows, bands), F32),
            grid_spec=pltpu.PrefetchScalarGridSpec(
                num_scalar_prefetch=1,
                grid=(n_x,),
                in_specs=[
                    pl.BlockSpec(
                        (1, 1, 1, share_rows, part), lambda i, c, p=p: (p, i, c[0], 0, 0)
                    )
                    for p in range(planes)
                ]
                + [pl.BlockSpec((bands, width), lambda i, c: (0, 0))],
                out_specs=pl.BlockSpec((1, share_rows, bands), lambda i, c: (i, 0, 0)),
            ),
            compiler_params=params(24),
            cost_estimate=cost(3),
            name="margin",
        )(side.reshape(1), *[by_plane] * planes, residual)

    given = lax.ppermute(margin_call(1 - core), "core", swap)
    pair = margin_call(core) + given
    share = pair.reshape(n_x, n_z, n_y, -1, bands).transpose(0, 2, 1, 3, 4)
    share = share.reshape(n_x * n_y, -1, bands)
    share = jnp.sum(lax.all_to_all(share, SHORT, 0, 0, tiled=True), axis=0)
    share = share.reshape(n_z, -1, bands)
    margins = jnp.sum(lax.all_to_all(share, "z", 0, 0, tiled=True), axis=0)

    coeffs = spread(margins.astype(BF16), "z").reshape(-1, bands)
    coeffs = spread(coeffs, SHORT).reshape(n_x, n_y, n_z, -1, bands)
    coeffs = coeffs.transpose(0, 2, 1, 3, 4).reshape(n_x, share_rows, bands)
    other = lax.ppermute(coeffs, "core", swap)
    whole_block = pl.BlockSpec((n_x, share_rows, bands), lambda p, c: (0, 0, 0))
    orthogonal = pl.pallas_call(
        clean_kernel,
        out_shape=jax.ShapeDtypeStruct((planes, bands, part), BF16),
        grid_spec=pltpu.PrefetchScalarGridSpec(
            num_scalar_prefetch=1,
            grid=(planes,),
            in_specs=[
                pl.BlockSpec((1, 1, 2, share_rows, part), lambda p, c, i=i: (p, i, 0, 0, 0))
                for i in range(n_x)
            ]
            + [
                whole_block,
                whole_block,
                pl.BlockSpec((bands, part), lambda p, c: (0, p)),
            ],
            out_specs=pl.BlockSpec((1, bands, part), lambda p, c: (p, 0, 0)),
            scratch_shapes=[pltpu.VMEM((2, n_x, bands, share_rows), BF16)],
        ),
        compiler_params=params(24),
        cost_estimate=cost(5),
        name="clean",
    )(core.reshape(1), *[by_plane] * n_x, coeffs, other, residual)
    return orthogonal.transpose(1, 0, 2), margins


def solution(mesh):
    n_band, n_dom = mesh.devices.shape
    n_y = 4 if n_dom % 4 == 0 else 2
    fine = Mesh(
        mesh.devices.reshape(n_band // 2, 2, n_dom // n_y, n_y), ("x", "core", "z", "y")
    )
    in_specs = (
        P(BAND, DOM, None, None),
        P(DOM, None, None),
        P(DOM, None),
        P(DOM),
        P(DOM),
        P(DOM),
        P(DOM),
        P(None, DOM, BAND),
    )
    out_specs = (P(None, DOM, BAND), P(BAND + DOM, None))
    return jax.shard_map(
        per_device, mesh=fine, in_specs=in_specs, out_specs=out_specs, check_vma=False
    )
```

```python
import functools

import jax
import jax.numpy as jnp
import numpy as np
from jax import lax
from jax.experimental import pallas as pl
from jax.experimental.pallas import tpu as pltpu
from jax.sharding import Mesh
from jax.sharding import PartitionSpec as P

BS = 128

COEFFS = (
    -5369.0 / 1800.0,
    12.0 / 7.0,
    -15.0 / 56.0,
    10.0 / 189.0,
    -1.0 / 112.0,
    2.0 / 825.0,
    -1.0 / 5544.0,
)
HALF = tuple(-0.5 * c for c in COEFFS)
WIDTH = 6
DOM = ("z", "y")
BAND = ("x", "core")
SHORT = ("x", "y")
F32 = jnp.float32
BF16 = jnp.bfloat16
VMEM = pl.BlockSpec(memory_space=pltpu.VMEM)
SMEM = pl.BlockSpec(memory_space=pltpu.SMEM)
ANY = pl.BlockSpec(memory_space=pl.ANY)


def params(mib):
    return pltpu.CompilerParams(vmem_limit_bytes=mib * 1024 * 1024)


def cost(microseconds):
    return pl.CostEstimate(
        flops=0, transcendentals=0, bytes_accessed=int(microseconds * 3_000_000)
    )


@functools.lru_cache
def plane_weights(width_y):
    src = np.arange(1024)
    dst = np.arange(256)
    dz = np.abs((src // width_y - 2 * (384 // (2 * width_y)))[:, None] - (dst // width_y)[None])
    dy = np.abs((src % width_y)[:, None] - (dst % width_y)[None])
    dy = np.minimum(dy, width_y - dy)
    table = np.zeros(2048)
    table[1 : WIDTH + 1] = HALF[1:]
    full = np.where(dy == 0, table[dz], 0.0) + np.where(dz == 0, table[dy], 0.0)
    terms = []
    for _ in range(3):
        term = full.astype(np.float32).astype(BF16)
        terms.append(term)
        full = full - term.astype(np.float64)
    return np.stack(terms)


def inner_kernel(block_ref, place_ref, x_ref, proj_ref, onehot_ref, share_ref, out_ref):
    for i in range(out_ref.shape[0]):
        out_ref[i] = place_ref[i]
    rows = x_ref.shape[0]
    slots = proj_ref.shape[0]
    lane = lax.broadcasted_iota(jnp.int32, (rows, BS), 1)

    def body(s, acc):
        start = pl.multiple_of(block_ref[s] * BS, BS)
        cells = x_ref[:, pl.ds(start, BS)].astype(F32)
        total = jnp.sum(cells * proj_ref[pl.ds(s, 1), :], axis=1, keepdims=True)
        return jnp.where(lane == s, total, acc)

    acc = lax.fori_loop(0, slots, body, jnp.zeros((rows, BS), F32), unroll=8)
    share_ref[...] = jnp.dot(
        acc, onehot_ref[...], precision=lax.Precision.HIGHEST, preferred_element_type=F32
    )


def local_kernel(planes, x_ref, pot_ref, w_ref, out_ref, den_ref, pad_ref):
    rows = x_ref.shape[0]
    plane = x_ref.shape[1] // planes
    zeros = jnp.zeros((planes * rows, 384), BF16)
    pad_ref[:, :384] = zeros
    pad_ref[:, 384 + plane :] = zeros
    for p in range(planes):
        pad_ref[p * rows : (p + 1) * rows, 384 : 384 + plane] = x_ref[:, p * plane : (p + 1) * plane]

    def body(step, den):
        start = pl.multiple_of(step * 256, 256)
        window = pad_ref[:, pl.ds(start, 1024)]
        acc = jnp.dot(window, w_ref[0], preferred_element_type=F32)
        acc += jnp.dot(window, w_ref[1], preferred_element_type=F32)
        acc += jnp.dot(window, w_ref[2], preferred_element_type=F32)
        mid = [window[p * rows : (p + 1) * rows, 384:640].astype(F32) for p in range(planes)]
        for p in range(planes):
            where = pl.multiple_of(p * plane + start, 256)
            value = acc[p * rows : (p + 1) * rows]
            value += (pot_ref[:, pl.ds(where, 256)] + 3.0 * HALF[0]) * mid[p]
            for q in range(planes):
                if q != p and abs(q - p) <= WIDTH:
                    value += HALF[abs(q - p)] * mid[q]
            out_ref[:, pl.ds(where, 256)] = value
            square = mid[p] * mid[p]
            den += square[:, :BS] + square[:, BS:]
        return den

    den_ref[...] = lax.fori_loop(0, plane // 256, body, jnp.zeros((rows, BS), F32))


def hamilton_kernel(
    planes,
    h0_ref,
    x_hbm,
    left_hbm,
    right_hbm,
    den_ref,
    mine_ref,
    coupling_ref,
    below_hbm,
    above_hbm,
    h_ref,
    pay_ref,
    x_ref,
    left_ref,
    right_ref,
    below_ref,
    above_ref,
    sems,
    late_sems,
):
    rows, cells = x_ref.shape
    plane = cells // planes
    chunks = sems.shape[0]
    chunk = plane // chunks
    copies = []
    for k in range(chunks):
        for p in range(planes):
            where = slice(p * plane + k * chunk, p * plane + (k + 1) * chunk)
            for i, (src, dst) in enumerate(
                ((x_hbm, x_ref), (left_hbm, left_ref), (right_hbm, right_ref))
            ):
                copies.append(
                    pltpu.make_async_copy(src.at[:, where], dst.at[:, where], sems.at[k, p, i])
                )
    late = [
        pltpu.make_async_copy(below_hbm, below_ref, late_sems.at[0]),
        pltpu.make_async_copy(above_hbm, above_ref, late_sems.at[1]),
    ]
    for copy in copies + late:
        copy.start()
    n = BS // 4

    def halo(step, carry):
        sums = []
        for top in range(0, rows, 16):
            pick = slice(top, top + 16)
            before = []
            after = []
            num = carry[top // 16]
            for p in range(planes):
                where = pl.ds(pl.multiple_of(p * plane + step * BS, BS), BS)
                before.append(left_ref[pick, where].astype(F32))
                after.append(right_ref[pick, where].astype(F32))
            for p in range(planes):
                where = pl.ds(pl.multiple_of(p * plane + step * BS, BS), BS)
                value = h0_ref[pick, where]
                for j in range(p, planes):
                    value += HALF[planes + p - j] * before[j]
                for j in range(p + 1):
                    value += HALF[planes + j - p] * after[j]
                h_ref[pick, where] = value
                num += value * x_ref[pick, where].astype(F32)
            sums.append(num)
        return tuple(sums)

    zero = jnp.zeros((16, BS), F32)
    num = (zero,) * (rows // 16)
    steps = chunk // BS
    for k in range(chunks):
        for copy in copies[k * planes * 3 : (k + 1) * planes * 3]:
            copy.wait()
        num = lax.fori_loop(k * steps, (k + 1) * steps, halo, num)
    num = jnp.concatenate(num, axis=0)

    for copy in late:
        copy.wait()
    lane = lax.broadcasted_iota(jnp.int32, (rows, BS), 1)
    row = lax.broadcasted_iota(jnp.int32, (rows, BS), 0)
    total = mine_ref[...]
    total += pltpu.roll(below_ref[...], 3 * n, 1)
    total += pltpu.roll(above_ref[...], n, 1)
    table = total * coupling_ref[...]
    num = jnp.sum(num + table * total, axis=1, keepdims=True)
    den = jnp.sum(den_ref[...], axis=1, keepdims=True)
    line = jnp.where(lane == row, num, 0.0) + jnp.where(lane == row + rows, den, 0.0)
    line = jnp.sum(line, axis=0, keepdims=True)

    short = rows // 4
    packed = None
    for g in range(4):
        piece = table[g * short : (g + 1) * short]
        piece = piece if g == 1 else pltpu.roll(piece, (g + 3) % 4 * n, 1)
        packed = piece if packed is None else packed + piece
    for r in range(short):
        pay_ref[:, r] = jnp.broadcast_to(packed[r : r + 1][None], (pay_ref.shape[0], 1, BS))
    pay_ref[:, short] = jnp.broadcast_to(line[None], (pay_ref.shape[0], 1, BS))


def residual_kernel(
    planes,
    block_ref,
    place_ref,
    h_ref,
    x_hbm,
    pay_ref,
    proj_hbm,
    onehot_hbm,
    r_ref,
    full_ref,
    x_ref,
    proj_ref,
    onehot_ref,
    sems,
):
    rows, cells = x_ref.shape
    plane = cells // planes
    copies = []
    for p in range(planes):
        where = slice(p * plane, (p + 1) * plane)
        copies.append(
            pltpu.make_async_copy(x_hbm.at[:, where], x_ref.at[:, where], sems.at[2 + p])
        )
    late = [
        pltpu.make_async_copy(proj_hbm, proj_ref, sems.at[0]),
        pltpu.make_async_copy(onehot_hbm, onehot_ref, sems.at[1]),
    ]
    for copy in copies + late:
        copy.start()
    slots = proj_ref.shape[0]
    n = BS // 4
    short = rows // 4
    lane = lax.broadcasted_iota(jnp.int32, (rows, BS), 1)
    row = lax.broadcasted_iota(jnp.int32, (rows, BS), 0)
    sums = jnp.sum(pay_ref[:, short], axis=0)
    num = jnp.sum(jnp.where(lane == row, sums, 0.0), axis=1, keepdims=True)
    den = jnp.sum(jnp.where(lane == row + rows, sums, 0.0), axis=1, keepdims=True)
    energy = jnp.broadcast_to(num / den, (rows, BS))
    for at in range(0, cells, BS):
        if at % plane == 0:
            copies[at // plane].wait()
        where = slice(at, at + BS)
        full_ref[:, where] = h_ref[:, where] - energy * x_ref[:, where].astype(F32)

    table = jnp.zeros((rows, BS), F32)
    for section in range(3):
        packed = jnp.concatenate(
            [pay_ref[place_ref[section], r] for r in range(short)], axis=0
        )
        pieces = [
            packed if g == section else pltpu.roll(packed, (section - g) % 4 * n, 1)
            for g in range(4)
        ]
        whole = jnp.concatenate(pieces, axis=0)
        table += jnp.where((lane >= section * n) & (lane < (section + 1) * n), whole, 0.0)
    for copy in late:
        copy.wait()
    value = lax.dot_general(
        table,
        onehot_ref[...],
        (((1,), (1,)), ((), ())),
        precision=lax.Precision.HIGHEST,
        preferred_element_type=F32,
    )
    for s in range(slots):
        where = pl.ds(pl.multiple_of(block_ref[s] * BS, BS), BS)
        full_ref[:, where] += value[:, s : s + 1] * proj_ref[s : s + 1, :]

    parts = r_ref.shape[0]
    part = plane // parts
    for c in range(parts):
        for p in range(planes):
            src = p * plane + c * part
            r_ref[c, :, p * part : (p + 1) * part] = full_ref[:, src : src + part].astype(BF16)


def margin_kernel(side, place_ref, locked_ref, r_ref, out_ref):
    planes, n_x, _, _, part = locked_ref.shape
    core = place_ref[3 + side]
    for i in range(n_x):
        acc = None
        for p in range(planes):
            term = lax.dot_general(
                locked_ref[p, i, core],
                r_ref[:, p * part : (p + 1) * part],
                (((1,), (1,)), ((), ())),
                preferred_element_type=F32,
            )
            acc = term if acc is None else acc + term
        out_ref[i] = acc


def pair_kernel(kept_ref, given_ref, out_ref):
    n_x, share_rows, _ = kept_ref.shape
    n_y = out_ref.shape[0] // n_x
    for i in range(n_x):
        for at in range(0, share_rows, 8):
            z, y = divmod(at // 8, n_y)
            out_ref[i * n_y + y, z * 8 : z * 8 + 8] = (
                kept_ref[i, at : at + 8] + given_ref[i, at : at + 8]
            )


def sum_kernel(in_ref, out_ref):
    acc = in_ref[0]
    for i in range(1, in_ref.shape[0]):
        acc += in_ref[i]
    out_ref[...] = acc


def clean_kernel(side, place_ref, locked_ref, coeff_ref, r_ref, out_ref, turned_ref):
    planes, n_x, _, share_rows, part = locked_ref.shape
    n_y = coeff_ref.shape[0] // n_x
    core = place_ref[3 + side]
    for i in range(n_x):
        pieces = [coeff_ref[i * n_y + y].astype(F32) for y in range(n_y)]
        whole = [
            pieces[at % n_y][at // n_y * 8 : at // n_y * 8 + 8] for at in range(share_rows // 8)
        ]
        turned_ref[i] = jnp.concatenate(whole, axis=0).T.astype(BF16)
    for p in range(planes):
        term = None
        for i in range(n_x):
            more = jnp.dot(turned_ref[i], locked_ref[p, i, core], preferred_element_type=F32)
            term = more if term is None else term + more
        if side == 0:
            out_ref[p] = r_ref[:, p * part : (p + 1) * part].astype(F32) - term
        else:
            out_ref[p] = (r_ref[p] - term).astype(BF16)


def ring(size):
    up = [(i, (i + 1) % size) for i in range(size)]
    return up, [(j, i) for i, j in up]


def spread(value, axis):
    size = lax.axis_size(axis)
    return lax.all_to_all(
        jnp.broadcast_to(value[None], (size,) + value.shape), axis, 0, 0, tiled=True
    )


def per_device(
    orbitals, potential, projectors, coupling, slot_block, slot_projector, slot_count, locked
):
    rows, planes, depth_z, width_y = orbitals.shape
    plane = depth_z * width_y
    cells = planes * plane
    domains = lax.axis_size(DOM)
    groups = lax.axis_size(BAND)
    n_x = lax.axis_size("x")
    n_z = lax.axis_size("z")
    n_y = lax.axis_size("y")
    core = lax.axis_index("core").astype(jnp.int32)
    here = lax.axis_index(DOM)
    slots = slot_block.shape[0]
    n = coupling.shape[0]
    part = plane // groups
    width = planes * part
    n_locked = locked.shape[0]
    bands = groups * rows
    share_rows = n_locked // groups
    up, down = ring(domains)
    swap = [(0, 1), (1, 0)]

    x = orbitals.reshape(rows, cells)
    left = lax.ppermute(x, DOM, up)
    right = lax.ppermute(x, DOM, down)

    pot = potential.reshape(1, cells)
    weights = jnp.asarray(plane_weights(width_y))
    active = jnp.arange(slots, dtype=jnp.int32) < slot_count[0]
    relative = (slot_projector // n - here + domains) % domains
    section = jnp.where(relative == 0, 1, jnp.where(relative == 1, 2, 0))
    column = section * n + slot_projector % n
    column = jnp.where(active, column, BS)
    column = jnp.pad(column, (0, BS - slots), constant_values=BS)
    onehot = (column[:, None] == jnp.arange(BS, dtype=jnp.int32)[None, :]).astype(F32)
    coupling_row = jnp.pad(coupling[None], ((0, 0), (n, BS - 2 * n)))

    near = (here + domains + jnp.arange(-1, 2, dtype=jnp.int32)) % domains
    place = jnp.concatenate([near, jnp.stack([core, 1 - core]), jnp.zeros(3, jnp.int32)])
    shares, place = pl.pallas_call(
        inner_kernel,
        out_shape=(
            jax.ShapeDtypeStruct((rows, BS), F32),
            jax.ShapeDtypeStruct((8,), jnp.int32),
        ),
        in_specs=[SMEM, SMEM, VMEM, VMEM, VMEM],
        out_specs=(VMEM, SMEM),
        compiler_params=params(8),
        cost_estimate=cost(2),
        name="inner",
    )(slot_block, place.astype(jnp.int32), x, projectors, onehot)
    x_hbm = pltpu.with_memory_space_constraint(x, pltpu.HBM)
    below = lax.ppermute(shares, DOM, up)
    above = lax.ppermute(shares, DOM, down)

    h0, den = pl.pallas_call(
        functools.partial(local_kernel, planes),
        out_shape=(
            jax.ShapeDtypeStruct((rows, cells), F32),
            jax.ShapeDtypeStruct((rows, BS), F32),
        ),
        in_specs=[VMEM, VMEM, VMEM],
        out_specs=(VMEM, VMEM),
        scratch_shapes=[pltpu.VMEM((planes * rows, plane + 768), BF16)],
        compiler_params=params(24),
        cost_estimate=cost(7),
        name="local",
    )(x, pot, weights)

    hamilton, pay = pl.pallas_call(
        functools.partial(hamilton_kernel, planes),
        out_shape=(
            jax.ShapeDtypeStruct((rows, cells), F32),
            jax.ShapeDtypeStruct((domains, rows // 4 + 1, 1, BS), F32),
        ),
        in_specs=[VMEM] + [ANY] * 3 + [VMEM] * 3 + [ANY] * 2,
        out_specs=(VMEM, VMEM),
        scratch_shapes=[pltpu.VMEM((rows, cells), BF16)] * 3
        + [pltpu.VMEM((rows, BS), F32)] * 2
        + [pltpu.SemaphoreType.DMA((3, planes, 3)), pltpu.SemaphoreType.DMA((2,))],
        compiler_params=params(24),
        cost_estimate=cost(5),
        name="hamilton",
    )(h0, x_hbm, left, right, den, shares, coupling_row, below, above)
    pay = lax.all_to_all(pay, DOM, 0, 0, tiled=True)

    residual = pl.pallas_call(
        functools.partial(residual_kernel, planes),
        out_shape=jax.ShapeDtypeStruct((groups, rows, width), BF16),
        in_specs=[SMEM, SMEM, VMEM, ANY, VMEM, ANY, ANY],
        out_specs=VMEM,
        scratch_shapes=[
            pltpu.VMEM((rows, cells), F32),
            pltpu.VMEM((rows, cells), BF16),
            pltpu.VMEM((slots, BS), F32),
            pltpu.VMEM((BS, BS), F32),
            pltpu.SemaphoreType.DMA((2 + planes,)),
        ],
        compiler_params=params(24),
        cost_estimate=cost(2),
        name="residual",
    )(slot_block, place, hamilton, x_hbm, pay, projectors, onehot)
    residual = lax.all_to_all(residual, BAND, 0, 0, tiled=True).reshape(bands, width)

    by_plane = locked.transpose(1, 0, 2).reshape(planes, n_x, 2, share_rows, part)
    by_plane = pltpu.with_memory_space_constraint(by_plane, pltpu.VMEM)

    def margin_call(side):
        return pl.pallas_call(
            functools.partial(margin_kernel, side),
            out_shape=jax.ShapeDtypeStruct((n_x, share_rows, bands), F32),
            in_specs=[SMEM, VMEM, VMEM],
            out_specs=VMEM,
            compiler_params=params(8),
            cost_estimate=cost(3),
            name="margin",
        )(place, by_plane, residual)

    def small_call(kernel, shape, name, *operands):
        return pl.pallas_call(
            kernel,
            out_shape=jax.ShapeDtypeStruct(shape, F32),
            in_specs=[VMEM] * len(operands),
            out_specs=VMEM,
            compiler_params=params(8),
            cost_estimate=cost(1),
            name=name,
        )(*operands)

    given = lax.ppermute(margin_call(1), "core", swap)
    kept = margin_call(0)
    share = small_call(pair_kernel, (n_x * n_y, n_z * 8, bands), "pair", kept, given)
    share = lax.all_to_all(share, SHORT, 0, 0, tiled=True)
    share = small_call(sum_kernel, (n_z * 8, bands), "sum", share).reshape(n_z, 8, bands)
    margins = lax.all_to_all(share, "z", 0, 0, tiled=True)
    margins = small_call(sum_kernel, (8, bands), "sum", margins)

    coeffs = spread(margins.astype(BF16), "z").reshape(n_z * 8, bands)
    coeffs = spread(coeffs, SHORT).reshape(n_x * n_y, n_z * 8, bands)
    other = lax.ppermute(coeffs, "core", swap)

    def clean_call(side, coeffs, before, kind):
        return pl.pallas_call(
            functools.partial(clean_kernel, side),
            out_shape=jax.ShapeDtypeStruct((planes, bands, part), kind),
            in_specs=[SMEM, VMEM, VMEM, VMEM],
            out_specs=VMEM,
            scratch_shapes=[pltpu.VMEM((n_x, bands, share_rows), BF16)],
            compiler_params=params(8),
            cost_estimate=cost(3),
            name="clean",
        )(place, by_plane, coeffs, before)

    part_clean = clean_call(0, coeffs, residual, F32)
    orthogonal = clean_call(1, other, part_clean, BF16)
    return orthogonal.transpose(1, 0, 2), margins


def solution(mesh):
    n_band, n_dom = mesh.devices.shape
    n_y = 4 if n_dom % 4 == 0 else 2
    fine = Mesh(
        mesh.devices.reshape(n_band // 2, 2, n_dom // n_y, n_y), ("x", "core", "z", "y")
    )
    in_specs = (
        P(BAND, DOM, None, None),
        P(DOM, None, None),
        P(DOM, None),
        P(DOM),
        P(DOM),
        P(DOM),
        P(DOM),
        P(None, DOM, BAND),
    )
    out_specs = (P(None, DOM, BAND), P(BAND + DOM, None))
    return jax.shard_map(
        per_device, mesh=fine, in_specs=in_specs, out_specs=out_specs, check_vma=False
    )
```

```python
import functools

import jax
import jax.numpy as jnp
import numpy as np
from jax import lax
from jax.experimental import pallas as pl
from jax.experimental.pallas import tpu as pltpu
from jax.sharding import Mesh
from jax.sharding import PartitionSpec as P

BS = 128

COEFFS = (
    -5369.0 / 1800.0,
    12.0 / 7.0,
    -15.0 / 56.0,
    10.0 / 189.0,
    -1.0 / 112.0,
    2.0 / 825.0,
    -1.0 / 5544.0,
)
HALF = tuple(-0.5 * c for c in COEFFS)
WIDTH = 6
DOM = ("z", "y")
BAND = ("x", "core")
SHORT = ("x", "y")
F32 = jnp.float32
BF16 = jnp.bfloat16
VMEM = pl.BlockSpec(memory_space=pltpu.VMEM)
SMEM = pl.BlockSpec(memory_space=pltpu.SMEM)
ANY = pl.BlockSpec(memory_space=pl.ANY)


def params(mib):
    return pltpu.CompilerParams(vmem_limit_bytes=mib * 1024 * 1024)


def cost(microseconds):
    return pl.CostEstimate(
        flops=0, transcendentals=0, bytes_accessed=int(microseconds * 3_000_000)
    )


@functools.lru_cache
def plane_weights(width_y):
    src = np.arange(1024)
    dst = np.arange(256)
    dz = np.abs((src // width_y - 2 * (384 // (2 * width_y)))[:, None] - (dst // width_y)[None])
    dy = np.abs((src % width_y)[:, None] - (dst % width_y)[None])
    dy = np.minimum(dy, width_y - dy)
    table = np.zeros(2048)
    table[1 : WIDTH + 1] = HALF[1:]
    full = np.where(dy == 0, table[dz], 0.0) + np.where(dz == 0, table[dy], 0.0)
    terms = []
    for _ in range(3):
        term = full.astype(np.float32).astype(BF16)
        terms.append(term)
        full = full - term.astype(np.float64)
    return np.stack(terms)


def inner_kernel(block_ref, place_ref, x_ref, proj_ref, onehot_ref, share_ref, out_ref):
    for i in range(out_ref.shape[0]):
        out_ref[i] = place_ref[i]
    rows = x_ref.shape[0]
    slots = proj_ref.shape[0]
    lane = lax.broadcasted_iota(jnp.int32, (rows, BS), 1)

    def body(s, acc):
        start = pl.multiple_of(block_ref[s] * BS, BS)
        cells = x_ref[:, pl.ds(start, BS)].astype(F32)
        total = jnp.sum(cells * proj_ref[pl.ds(s, 1), :], axis=1, keepdims=True)
        return jnp.where(lane == s, total, acc)

    acc = lax.fori_loop(0, slots, body, jnp.zeros((rows, BS), F32), unroll=8)
    share_ref[...] = jnp.dot(
        acc, onehot_ref[...], precision=lax.Precision.HIGHEST, preferred_element_type=F32
    )


def local_kernel(planes, x_ref, pot_ref, w_ref, out_ref, den_ref, pad_ref):
    rows = x_ref.shape[0]
    plane = x_ref.shape[1] // planes
    zeros = jnp.zeros((planes * rows, 384), BF16)
    pad_ref[:, :384] = zeros
    pad_ref[:, 384 + plane :] = zeros
    for p in range(planes):
        pad_ref[p * rows : (p + 1) * rows, 384 : 384 + plane] = x_ref[:, p * plane : (p + 1) * plane]

    def body(step, den):
        start = pl.multiple_of(step * 256, 256)
        window = pad_ref[:, pl.ds(start, 1024)]
        acc = jnp.dot(window, w_ref[0], preferred_element_type=F32)
        acc += jnp.dot(window, w_ref[1], preferred_element_type=F32)
        acc += jnp.dot(window, w_ref[2], preferred_element_type=F32)
        mid = [window[p * rows : (p + 1) * rows, 384:640].astype(F32) for p in range(planes)]
        for p in range(planes):
            where = pl.multiple_of(p * plane + start, 256)
            value = acc[p * rows : (p + 1) * rows]
            value += (pot_ref[:, pl.ds(where, 256)] + 3.0 * HALF[0]) * mid[p]
            for q in range(planes):
                if q != p and abs(q - p) <= WIDTH:
                    value += HALF[abs(q - p)] * mid[q]
            out_ref[:, pl.ds(where, 256)] = value
            square = mid[p] * mid[p]
            den += square[:, :BS] + square[:, BS:]
        return den

    den_ref[...] = lax.fori_loop(0, plane // 256, body, jnp.zeros((rows, BS), F32))


def hamilton_kernel(
    planes,
    h0_ref,
    x_hbm,
    left_hbm,
    right_hbm,
    den_ref,
    mine_ref,
    coupling_ref,
    below_hbm,
    above_hbm,
    h_ref,
    pay_ref,
    x_ref,
    left_ref,
    right_ref,
    below_ref,
    above_ref,
    sems,
    late_sems,
):
    rows, cells = x_ref.shape
    plane = cells // planes
    chunks = sems.shape[0]
    chunk = plane // chunks
    copies = []
    for k in range(chunks):
        for p in range(planes):
            where = slice(p * plane + k * chunk, p * plane + (k + 1) * chunk)
            for i, (src, dst) in enumerate(
                ((x_hbm, x_ref), (left_hbm, left_ref), (right_hbm, right_ref))
            ):
                copies.append(
                    pltpu.make_async_copy(src.at[:, where], dst.at[:, where], sems.at[k, p, i])
                )
    late = [
        pltpu.make_async_copy(below_hbm, below_ref, late_sems.at[0]),
        pltpu.make_async_copy(above_hbm, above_ref, late_sems.at[1]),
    ]
    for copy in copies + late:
        copy.start()
    n = BS // 4

    def halo(step, carry):
        sums = []
        for top in range(0, rows, 16):
            pick = slice(top, top + 16)
            before = []
            after = []
            num = carry[top // 16]
            for p in range(planes):
                where = pl.ds(pl.multiple_of(p * plane + step * BS, BS), BS)
                before.append(left_ref[pick, where].astype(F32))
                after.append(right_ref[pick, where].astype(F32))
            for p in range(planes):
                where = pl.ds(pl.multiple_of(p * plane + step * BS, BS), BS)
                value = h0_ref[pick, where]
                for j in range(p, planes):
                    value += HALF[planes + p - j] * before[j]
                for j in range(p + 1):
                    value += HALF[planes + j - p] * after[j]
                h_ref[pick, where] = value
                num += value * x_ref[pick, where].astype(F32)
            sums.append(num)
        return tuple(sums)

    zero = jnp.zeros((16, BS), F32)
    num = (zero,) * (rows // 16)
    steps = chunk // BS
    for k in range(chunks):
        for copy in copies[k * planes * 3 : (k + 1) * planes * 3]:
            copy.wait()
        num = lax.fori_loop(k * steps, (k + 1) * steps, halo, num)
    num = jnp.concatenate(num, axis=0)

    for copy in late:
        copy.wait()
    lane = lax.broadcasted_iota(jnp.int32, (rows, BS), 1)
    row = lax.broadcasted_iota(jnp.int32, (rows, BS), 0)
    total = mine_ref[...]
    total += pltpu.roll(below_ref[...], 3 * n, 1)
    total += pltpu.roll(above_ref[...], n, 1)
    table = total * coupling_ref[...]
    num = jnp.sum(num + table * total, axis=1, keepdims=True)
    den = jnp.sum(den_ref[...], axis=1, keepdims=True)
    line = jnp.where(lane == row, num, 0.0) + jnp.where(lane == row + rows, den, 0.0)
    line = jnp.sum(line, axis=0, keepdims=True)

    short = rows // 4
    packed = None
    for g in range(4):
        piece = table[g * short : (g + 1) * short]
        piece = piece if g == 1 else pltpu.roll(piece, (g + 3) % 4 * n, 1)
        packed = piece if packed is None else packed + piece
    for r in range(short):
        pay_ref[:, r] = jnp.broadcast_to(packed[r : r + 1][None], (pay_ref.shape[0], 1, BS))
    pay_ref[:, short] = jnp.broadcast_to(line[None], (pay_ref.shape[0], 1, BS))


def residual_kernel(
    planes,
    block_ref,
    place_ref,
    h_ref,
    x_hbm,
    pay_ref,
    proj_hbm,
    onehot_hbm,
    r_ref,
    full_ref,
    x_ref,
    proj_ref,
    onehot_ref,
    sems,
):
    rows, cells = x_ref.shape
    plane = cells // planes
    copies = []
    for p in range(planes):
        where = slice(p * plane, (p + 1) * plane)
        copies.append(
            pltpu.make_async_copy(x_hbm.at[:, where], x_ref.at[:, where], sems.at[2 + p])
        )
    late = [
        pltpu.make_async_copy(proj_hbm, proj_ref, sems.at[0]),
        pltpu.make_async_copy(onehot_hbm, onehot_ref, sems.at[1]),
    ]
    for copy in copies + late:
        copy.start()
    slots = proj_ref.shape[0]
    n = BS // 4
    short = rows // 4
    lane = lax.broadcasted_iota(jnp.int32, (rows, BS), 1)
    row = lax.broadcasted_iota(jnp.int32, (rows, BS), 0)
    sums = jnp.sum(pay_ref[:, short], axis=0)
    num = jnp.sum(jnp.where(lane == row, sums, 0.0), axis=1, keepdims=True)
    den = jnp.sum(jnp.where(lane == row + rows, sums, 0.0), axis=1, keepdims=True)
    energy = jnp.broadcast_to(num / den, (rows, BS))
    for at in range(0, cells, BS):
        if at % plane == 0:
            copies[at // plane].wait()
        where = slice(at, at + BS)
        full_ref[:, where] = h_ref[:, where] - energy * x_ref[:, where].astype(F32)

    table = jnp.zeros((rows, BS), F32)
    for section in range(3):
        packed = jnp.concatenate(
            [pay_ref[place_ref[section], r] for r in range(short)], axis=0
        )
        pieces = [
            packed if g == section else pltpu.roll(packed, (section - g) % 4 * n, 1)
            for g in range(4)
        ]
        whole = jnp.concatenate(pieces, axis=0)
        table += jnp.where((lane >= section * n) & (lane < (section + 1) * n), whole, 0.0)
    for copy in late:
        copy.wait()
    value = lax.dot_general(
        table,
        onehot_ref[...],
        (((1,), (1,)), ((), ())),
        precision=lax.Precision.HIGHEST,
        preferred_element_type=F32,
    )
    for s in range(slots):
        where = pl.ds(pl.multiple_of(block_ref[s] * BS, BS), BS)
        full_ref[:, where] += value[:, s : s + 1] * proj_ref[s : s + 1, :]

    parts = r_ref.shape[0]
    part = plane // parts
    for c in range(parts):
        for p in range(planes):
            src = p * plane + c * part
            r_ref[c, :, p * part : (p + 1) * part] = full_ref[:, src : src + part].astype(BF16)


def margin_kernel(side, place_ref, locked_ref, r_ref, out_ref):
    planes, n_x, _, _, part = locked_ref.shape
    core = place_ref[3 + side]
    for i in range(n_x):
        acc = None
        for p in range(planes):
            term = lax.dot_general(
                locked_ref[p, i, core],
                r_ref[:, p * part : (p + 1) * part],
                (((1,), (1,)), ((), ())),
                preferred_element_type=F32,
            )
            acc = term if acc is None else acc + term
        out_ref[i] = acc


def pair_kernel(kept_ref, given_ref, out_ref):
    n_x, share_rows, _ = kept_ref.shape
    n_y = out_ref.shape[0] // n_x
    for i in range(n_x):
        for y in range(n_y):
            pieces = [
                kept_ref[i, at : at + 8] + given_ref[i, at : at + 8]
                for at in range(y * 8, share_rows, n_y * 8)
            ]
            out_ref[i * n_y + y] = jnp.concatenate(pieces, axis=0).astype(BF16)


def sum_kernel(in_ref, out_ref, *copies):
    acc = in_ref[0].astype(F32)
    for i in range(1, in_ref.shape[0]):
        acc += in_ref[i].astype(F32)
    out_ref[...] = acc
    for ref in copies:
        for i in range(ref.shape[0]):
            ref[i] = acc


def copies_kernel(in_ref, out_ref):
    value = in_ref[...].astype(BF16)
    for i in range(out_ref.shape[0]):
        out_ref[i] = value


def clean_kernel(side, place_ref, locked_ref, coeff_ref, r_ref, out_ref, turned_ref):
    planes, n_x, _, share_rows, part = locked_ref.shape
    n_y = coeff_ref.shape[0] // n_x
    core = place_ref[3 + side]
    for i in range(n_x):
        pieces = [coeff_ref[i * n_y + y].astype(F32) for y in range(n_y)]
        whole = [
            pieces[at % n_y][at // n_y * 8 : at // n_y * 8 + 8] for at in range(share_rows // 8)
        ]
        turned_ref[i] = jnp.concatenate(whole, axis=0).T.astype(BF16)
    for p in range(planes):
        term = None
        for i in range(n_x):
            more = jnp.dot(turned_ref[i], locked_ref[p, i, core], preferred_element_type=F32)
            term = more if term is None else term + more
        if side == 0:
            out_ref[p] = r_ref[:, p * part : (p + 1) * part].astype(F32) - term
        else:
            out_ref[p] = (r_ref[p] - term).astype(BF16)


def ring(size):
    up = [(i, (i + 1) % size) for i in range(size)]
    return up, [(j, i) for i, j in up]


def per_device(
    orbitals, potential, projectors, coupling, slot_block, slot_projector, slot_count, locked
):
    rows, planes, depth_z, width_y = orbitals.shape
    plane = depth_z * width_y
    cells = planes * plane
    domains = lax.axis_size(DOM)
    groups = lax.axis_size(BAND)
    n_x = lax.axis_size("x")
    n_z = lax.axis_size("z")
    n_y = lax.axis_size("y")
    core = lax.axis_index("core").astype(jnp.int32)
    here = lax.axis_index(DOM)
    slots = slot_block.shape[0]
    n = coupling.shape[0]
    part = plane // groups
    width = planes * part
    n_locked = locked.shape[0]
    bands = groups * rows
    share_rows = n_locked // groups
    up, down = ring(domains)
    swap = [(0, 1), (1, 0)]

    x = orbitals.reshape(rows, cells)
    left = lax.ppermute(x, DOM, up)
    right = lax.ppermute(x, DOM, down)

    pot = potential.reshape(1, cells)
    weights = jnp.asarray(plane_weights(width_y))
    active = jnp.arange(slots, dtype=jnp.int32) < slot_count[0]
    relative = (slot_projector // n - here + domains) % domains
    section = jnp.where(relative == 0, 1, jnp.where(relative == 1, 2, 0))
    column = section * n + slot_projector % n
    column = jnp.where(active, column, BS)
    column = jnp.pad(column, (0, BS - slots), constant_values=BS)
    onehot = (column[:, None] == jnp.arange(BS, dtype=jnp.int32)[None, :]).astype(F32)
    coupling_row = jnp.pad(coupling[None], ((0, 0), (n, BS - 2 * n)))

    near = (here + domains + jnp.arange(-1, 2, dtype=jnp.int32)) % domains
    place = jnp.concatenate([near, jnp.stack([core, 1 - core]), jnp.zeros(3, jnp.int32)])
    shares, place = pl.pallas_call(
        inner_kernel,
        out_shape=(
            jax.ShapeDtypeStruct((rows, BS), F32),
            jax.ShapeDtypeStruct((8,), jnp.int32),
        ),
        in_specs=[SMEM, SMEM, VMEM, VMEM, VMEM],
        out_specs=(VMEM, SMEM),
        compiler_params=params(8),
        cost_estimate=cost(2),
        name="inner",
    )(slot_block, place.astype(jnp.int32), x, projectors, onehot)
    x_hbm = pltpu.with_memory_space_constraint(x, pltpu.HBM)
    below = lax.ppermute(shares, DOM, up)
    above = lax.ppermute(shares, DOM, down)

    h0, den = pl.pallas_call(
        functools.partial(local_kernel, planes),
        out_shape=(
            jax.ShapeDtypeStruct((rows, cells), F32),
            jax.ShapeDtypeStruct((rows, BS), F32),
        ),
        in_specs=[VMEM, VMEM, VMEM],
        out_specs=(VMEM, VMEM),
        scratch_shapes=[pltpu.VMEM((planes * rows, plane + 768), BF16)],
        compiler_params=params(24),
        cost_estimate=cost(7),
        name="local",
    )(x, pot, weights)

    hamilton, pay = pl.pallas_call(
        functools.partial(hamilton_kernel, planes),
        out_shape=(
            jax.ShapeDtypeStruct((rows, cells), F32),
            jax.ShapeDtypeStruct((domains, rows // 4 + 1, 1, BS), F32),
        ),
        in_specs=[VMEM] + [ANY] * 3 + [VMEM] * 3 + [ANY] * 2,
        out_specs=(VMEM, VMEM),
        scratch_shapes=[pltpu.VMEM((rows, cells), BF16)] * 3
        + [pltpu.VMEM((rows, BS), F32)] * 2
        + [pltpu.SemaphoreType.DMA((3, planes, 3)), pltpu.SemaphoreType.DMA((2,))],
        compiler_params=params(24),
        cost_estimate=cost(5),
        name="hamilton",
    )(h0, x_hbm, left, right, den, shares, coupling_row, below, above)
    pay = lax.all_to_all(pay, DOM, 0, 0, tiled=True)

    residual = pl.pallas_call(
        functools.partial(residual_kernel, planes),
        out_shape=jax.ShapeDtypeStruct((groups, rows, width), BF16),
        in_specs=[SMEM, SMEM, VMEM, ANY, VMEM, ANY, ANY],
        out_specs=VMEM,
        scratch_shapes=[
            pltpu.VMEM((rows, cells), F32),
            pltpu.VMEM((rows, cells), BF16),
            pltpu.VMEM((slots, BS), F32),
            pltpu.VMEM((BS, BS), F32),
            pltpu.SemaphoreType.DMA((2 + planes,)),
        ],
        compiler_params=params(24),
        cost_estimate=cost(2),
        name="residual",
    )(slot_block, place, hamilton, x_hbm, pay, projectors, onehot)
    residual = lax.all_to_all(residual, BAND, 0, 0, tiled=True).reshape(bands, width)

    by_plane = locked.transpose(1, 0, 2).reshape(planes, n_x, 2, share_rows, part)
    by_plane = pltpu.with_memory_space_constraint(by_plane, pltpu.VMEM)

    def margin_call(side):
        return pl.pallas_call(
            functools.partial(margin_kernel, side),
            out_shape=jax.ShapeDtypeStruct((n_x, share_rows, bands), F32),
            in_specs=[SMEM, VMEM, VMEM],
            out_specs=VMEM,
            compiler_params=params(8),
            cost_estimate=cost(3),
            name="margin",
        )(place, by_plane, residual)

    def small_call(kernel, shapes, name, *operands):
        return pl.pallas_call(
            kernel,
            out_shape=shapes,
            in_specs=[VMEM] * len(operands),
            out_specs=jax.tree.map(lambda _: VMEM, shapes),
            compiler_params=params(8),
            cost_estimate=cost(1),
            name=name,
        )(*operands)

    short = jax.ShapeDtypeStruct((n_x * n_y, n_z * 8, bands), BF16)
    whole = jax.ShapeDtypeStruct((n_z * 8, bands), F32)
    eighth = jax.ShapeDtypeStruct((8, bands), F32)
    given = lax.ppermute(margin_call(1), "core", swap)
    kept = margin_call(0)
    share = small_call(pair_kernel, short, "pair", kept, given)
    share = lax.all_to_all(share, SHORT, 0, 0, tiled=True)
    share = small_call(sum_kernel, whole, "sum", share).reshape(n_z, 8, bands)
    share = lax.all_to_all(share, "z", 0, 0, tiled=True)
    spread_out = jax.ShapeDtypeStruct((n_z, 8, bands), F32)
    margins, coeffs = small_call(sum_kernel, (eighth, spread_out), "sum", share)

    coeffs = lax.all_to_all(coeffs, "z", 0, 0, tiled=True).reshape(n_z * 8, bands)
    coeffs = small_call(copies_kernel, short, "copies", coeffs)
    coeffs = lax.all_to_all(coeffs, SHORT, 0, 0, tiled=True)
    other = lax.ppermute(coeffs, "core", swap)

    def clean_call(side, coeffs, before, kind):
        return pl.pallas_call(
            functools.partial(clean_kernel, side),
            out_shape=jax.ShapeDtypeStruct((planes, bands, part), kind),
            in_specs=[SMEM, VMEM, VMEM, VMEM],
            out_specs=VMEM,
            scratch_shapes=[pltpu.VMEM((n_x, bands, share_rows), BF16)],
            compiler_params=params(8),
            cost_estimate=cost(3),
            name="clean",
        )(place, by_plane, coeffs, before)

    part_clean = clean_call(0, coeffs, residual, F32)
    orthogonal = clean_call(1, other, part_clean, BF16)
    return orthogonal.transpose(1, 0, 2), margins


def solution(mesh):
    n_band, n_dom = mesh.devices.shape
    n_y = 4 if n_dom % 4 == 0 else 2
    fine = Mesh(
        mesh.devices.reshape(n_band // 2, 2, n_dom // n_y, n_y), ("x", "core", "z", "y")
    )
    in_specs = (
        P(BAND, DOM, None, None),
        P(DOM, None, None),
        P(DOM, None),
        P(DOM),
        P(DOM),
        P(DOM),
        P(DOM),
        P(None, DOM, BAND),
    )
    out_specs = (P(None, DOM, BAND), P(BAND + DOM, None))
    return jax.shard_map(
        per_device, mesh=fine, in_specs=in_specs, out_specs=out_specs, check_vma=False
    )
```

```python
import functools

import jax
import jax.numpy as jnp
import numpy as np
from jax import lax
from jax.experimental import pallas as pl
from jax.experimental.pallas import tpu as pltpu
from jax.sharding import Mesh
from jax.sharding import PartitionSpec as P

BS = 128

COEFFS = (
    -5369.0 / 1800.0,
    12.0 / 7.0,
    -15.0 / 56.0,
    10.0 / 189.0,
    -1.0 / 112.0,
    2.0 / 825.0,
    -1.0 / 5544.0,
)
HALF = tuple(-0.5 * c for c in COEFFS)
WIDTH = 6
DOM = ("z", "y")
BAND = ("x", "core")
SHORT = ("x", "y")
F32 = jnp.float32
BF16 = jnp.bfloat16
VMEM = pl.BlockSpec(memory_space=pltpu.VMEM)
SMEM = pl.BlockSpec(memory_space=pltpu.SMEM)
ANY = pl.BlockSpec(memory_space=pl.ANY)


def params(mib):
    return pltpu.CompilerParams(vmem_limit_bytes=mib * 1024 * 1024)


def cost(microseconds):
    return pl.CostEstimate(
        flops=0, transcendentals=0, bytes_accessed=int(microseconds * 3_000_000)
    )


@functools.lru_cache
def plane_weights(width_y):
    src = np.arange(1024)
    dst = np.arange(256)
    dz = np.abs((src // width_y - 2 * (384 // (2 * width_y)))[:, None] - (dst // width_y)[None])
    dy = np.abs((src % width_y)[:, None] - (dst % width_y)[None])
    dy = np.minimum(dy, width_y - dy)
    table = np.zeros(2048)
    table[1 : WIDTH + 1] = HALF[1:]
    full = np.where(dy == 0, table[dz], 0.0) + np.where(dz == 0, table[dy], 0.0)
    terms = []
    for _ in range(3):
        term = full.astype(np.float32).astype(BF16)
        terms.append(term)
        full = full - term.astype(np.float64)
    return np.stack(terms)


def inner_kernel(block_ref, place_ref, x_ref, proj_ref, onehot_ref, share_ref, out_ref):
    for i in range(out_ref.shape[0]):
        out_ref[i] = place_ref[i]
    rows = x_ref.shape[0]
    slots = proj_ref.shape[0]
    lane = lax.broadcasted_iota(jnp.int32, (rows, BS), 1)

    def body(s, acc):
        start = pl.multiple_of(block_ref[s] * BS, BS)
        cells = x_ref[:, pl.ds(start, BS)].astype(F32)
        total = jnp.sum(cells * proj_ref[pl.ds(s, 1), :], axis=1, keepdims=True)
        return jnp.where(lane == s, total, acc)

    acc = lax.fori_loop(0, slots, body, jnp.zeros((rows, BS), F32), unroll=8)
    share_ref[...] = jnp.dot(
        acc, onehot_ref[...], precision=lax.Precision.HIGHEST, preferred_element_type=F32
    )


def local_kernel(planes, x_ref, pot_ref, w_ref, out_ref, den_ref, pad_ref):
    rows = x_ref.shape[0]
    plane = x_ref.shape[1] // planes
    zeros = jnp.zeros((planes * rows, 384), BF16)
    pad_ref[:, :384] = zeros
    pad_ref[:, 384 + plane :] = zeros
    for p in range(planes):
        pad_ref[p * rows : (p + 1) * rows, 384 : 384 + plane] = x_ref[:, p * plane : (p + 1) * plane]

    def body(step, den):
        start = pl.multiple_of(step * 256, 256)
        window = pad_ref[:, pl.ds(start, 1024)]
        acc = jnp.dot(window, w_ref[0], preferred_element_type=F32)
        acc += jnp.dot(window, w_ref[1], preferred_element_type=F32)
        acc += jnp.dot(window, w_ref[2], preferred_element_type=F32)
        mid = [window[p * rows : (p + 1) * rows, 384:640].astype(F32) for p in range(planes)]
        for p in range(planes):
            where = pl.multiple_of(p * plane + start, 256)
            value = acc[p * rows : (p + 1) * rows]
            value += (pot_ref[:, pl.ds(where, 256)] + 3.0 * HALF[0]) * mid[p]
            for q in range(planes):
                if q != p and abs(q - p) <= WIDTH:
                    value += HALF[abs(q - p)] * mid[q]
            out_ref[:, pl.ds(where, 256)] = value
            square = mid[p] * mid[p]
            den += square[:, :BS] + square[:, BS:]
        return den

    den_ref[...] = lax.fori_loop(0, plane // 256, body, jnp.zeros((rows, BS), F32))


def hamilton_kernel(
    planes,
    h0_ref,
    x_ref,
    left_hbm,
    right_hbm,
    den_ref,
    mine_ref,
    coupling_ref,
    below_hbm,
    above_hbm,
    h_ref,
    pay_ref,
    left_ref,
    right_ref,
    below_ref,
    above_ref,
    sems,
    late_sems,
):
    rows, cells = x_ref.shape
    plane = cells // planes
    chunks = sems.shape[0]
    chunk = plane // chunks
    copies = []
    for k in range(chunks):
        for p in range(planes):
            where = slice(p * plane + k * chunk, p * plane + (k + 1) * chunk)
            for i, (src, dst) in enumerate(
                ((left_hbm, left_ref), (right_hbm, right_ref))
            ):
                copies.append(
                    pltpu.make_async_copy(src.at[:, where], dst.at[:, where], sems.at[k, p, i])
                )
    late = [
        pltpu.make_async_copy(below_hbm, below_ref, late_sems.at[0]),
        pltpu.make_async_copy(above_hbm, above_ref, late_sems.at[1]),
    ]
    for copy in copies + late:
        copy.start()
    n = BS // 4

    def halo(step, carry):
        sums = []
        for top in range(0, rows, 16):
            pick = slice(top, top + 16)
            before = []
            after = []
            num = carry[top // 16]
            for p in range(planes):
                where = pl.ds(pl.multiple_of(p * plane + step * BS, BS), BS)
                before.append(left_ref[pick, where].astype(F32))
                after.append(right_ref[pick, where].astype(F32))
            for p in range(planes):
                where = pl.ds(pl.multiple_of(p * plane + step * BS, BS), BS)
                value = h0_ref[pick, where]
                for j in range(p, planes):
                    value += HALF[planes + p - j] * before[j]
                for j in range(p + 1):
                    value += HALF[planes + j - p] * after[j]
                h_ref[pick, where] = value
                num += value * x_ref[pick, where].astype(F32)
            sums.append(num)
        return tuple(sums)

    zero = jnp.zeros((16, BS), F32)
    num = (zero,) * (rows // 16)
    steps = chunk // BS
    for k in range(chunks):
        for copy in copies[k * planes * 2 : (k + 1) * planes * 2]:
            copy.wait()
        num = lax.fori_loop(k * steps, (k + 1) * steps, halo, num)
    num = jnp.concatenate(num, axis=0)

    for copy in late:
        copy.wait()
    lane = lax.broadcasted_iota(jnp.int32, (rows, BS), 1)
    row = lax.broadcasted_iota(jnp.int32, (rows, BS), 0)
    total = mine_ref[...]
    total += pltpu.roll(below_ref[...], 3 * n, 1)
    total += pltpu.roll(above_ref[...], n, 1)
    table = total * coupling_ref[...]
    num = jnp.sum(num + table * total, axis=1, keepdims=True)
    den = jnp.sum(den_ref[...], axis=1, keepdims=True)
    line = jnp.where(lane == row, num, 0.0) + jnp.where(lane == row + rows, den, 0.0)
    line = jnp.sum(line, axis=0, keepdims=True)

    short = rows // 4
    packed = None
    for g in range(4):
        piece = table[g * short : (g + 1) * short]
        piece = piece if g == 1 else pltpu.roll(piece, (g + 3) % 4 * n, 1)
        packed = piece if packed is None else packed + piece
    for r in range(short):
        pay_ref[:, r] = jnp.broadcast_to(packed[r : r + 1][None], (pay_ref.shape[0], 1, BS))
    pay_ref[:, short] = jnp.broadcast_to(line[None], (pay_ref.shape[0], 1, BS))


def residual_kernel(
    planes,
    block_ref,
    place_ref,
    h_ref,
    x_ref,
    pay_ref,
    proj_hbm,
    onehot_hbm,
    r_ref,
    full_ref,
    proj_ref,
    onehot_ref,
    sems,
):
    rows, cells = x_ref.shape
    plane = cells // planes
    late = [
        pltpu.make_async_copy(proj_hbm, proj_ref, sems.at[0]),
        pltpu.make_async_copy(onehot_hbm, onehot_ref, sems.at[1]),
    ]
    for copy in late:
        copy.start()
    slots = proj_ref.shape[0]
    n = BS // 4
    short = rows // 4
    lane = lax.broadcasted_iota(jnp.int32, (rows, BS), 1)
    row = lax.broadcasted_iota(jnp.int32, (rows, BS), 0)
    sums = jnp.sum(pay_ref[:, short], axis=0)
    num = jnp.sum(jnp.where(lane == row, sums, 0.0), axis=1, keepdims=True)
    den = jnp.sum(jnp.where(lane == row + rows, sums, 0.0), axis=1, keepdims=True)
    energy = jnp.broadcast_to(num / den, (rows, BS))
    for at in range(0, cells, BS):
        where = slice(at, at + BS)
        full_ref[:, where] = h_ref[:, where] - energy * x_ref[:, where].astype(F32)

    table = jnp.zeros((rows, BS), F32)
    for section in range(3):
        packed = jnp.concatenate(
            [pay_ref[place_ref[section], r] for r in range(short)], axis=0
        )
        pieces = [
            packed if g == section else pltpu.roll(packed, (section - g) % 4 * n, 1)
            for g in range(4)
        ]
        whole = jnp.concatenate(pieces, axis=0)
        table += jnp.where((lane >= section * n) & (lane < (section + 1) * n), whole, 0.0)
    for copy in late:
        copy.wait()
    value = lax.dot_general(
        table,
        onehot_ref[...],
        (((1,), (1,)), ((), ())),
        precision=lax.Precision.HIGHEST,
        preferred_element_type=F32,
    )
    for s in range(slots):
        where = pl.ds(pl.multiple_of(block_ref[s] * BS, BS), BS)
        full_ref[:, where] += value[:, s : s + 1] * proj_ref[s : s + 1, :]

    parts = r_ref.shape[0]
    part = plane // parts
    for c in range(parts):
        for p in range(planes):
            src = p * plane + c * part
            r_ref[c, :, p * part : (p + 1) * part] = full_ref[:, src : src + part].astype(BF16)


def margin_kernel(side, place_ref, locked_ref, r_ref, out_ref):
    planes, n_x, _, _, part = locked_ref.shape
    core = place_ref[3 + side]
    for i in range(n_x):
        acc = None
        for p in range(planes):
            term = lax.dot_general(
                locked_ref[p, i, core],
                r_ref[:, p * part : (p + 1) * part],
                (((1,), (1,)), ((), ())),
                preferred_element_type=F32,
            )
            acc = term if acc is None else acc + term
        out_ref[i] = acc


def pair_kernel(kept_ref, given_ref, out_ref):
    n_x, share_rows, _ = kept_ref.shape
    n_y = out_ref.shape[0] // n_x
    for i in range(n_x):
        for y in range(n_y):
            pieces = [
                kept_ref[i, at : at + 8] + given_ref[i, at : at + 8]
                for at in range(y * 8, share_rows, n_y * 8)
            ]
            out_ref[i * n_y + y] = jnp.concatenate(pieces, axis=0).astype(BF16)


def partial_kernel(in_ref, out_ref):
    acc = in_ref[0].astype(F32)
    for i in range(1, in_ref.shape[0]):
        acc += in_ref[i].astype(F32)
    value = acc.astype(BF16)
    for i in range(out_ref.shape[0]):
        out_ref[i] = value


def total_kernel(place_ref, in_ref, margin_ref, coeff_ref, total_ref):
    acc = in_ref[0].astype(F32)
    for i in range(1, in_ref.shape[0]):
        acc += in_ref[i].astype(F32)
    total_ref[...] = acc
    value = acc.astype(BF16)
    for i in range(coeff_ref.shape[0]):
        coeff_ref[i] = value
    margin_ref[...] = total_ref[pl.ds(pl.multiple_of(place_ref[5] * 8, 8), 8)]


def clean_kernel(side, place_ref, locked_ref, coeff_ref, r_ref, out_ref, turned_ref):
    planes, n_x, _, share_rows, part = locked_ref.shape
    n_y = coeff_ref.shape[0] // n_x
    core = place_ref[3 + side]
    for i in range(n_x):
        pieces = [coeff_ref[i * n_y + y].astype(F32) for y in range(n_y)]
        whole = [
            pieces[at % n_y][at // n_y * 8 : at // n_y * 8 + 8] for at in range(share_rows // 8)
        ]
        turned_ref[i] = jnp.concatenate(whole, axis=0).T.astype(BF16)
    for p in range(planes):
        term = None
        for i in range(n_x):
            more = jnp.dot(turned_ref[i], locked_ref[p, i, core], preferred_element_type=F32)
            term = more if term is None else term + more
        if side == 0:
            out_ref[p] = r_ref[:, p * part : (p + 1) * part].astype(F32) - term
        else:
            out_ref[p] = (r_ref[p] - term).astype(BF16)


def ring(size):
    up = [(i, (i + 1) % size) for i in range(size)]
    return up, [(j, i) for i, j in up]


def per_device(
    orbitals, potential, projectors, coupling, slot_block, slot_projector, slot_count, locked
):
    rows, planes, depth_z, width_y = orbitals.shape
    plane = depth_z * width_y
    cells = planes * plane
    domains = lax.axis_size(DOM)
    groups = lax.axis_size(BAND)
    n_x = lax.axis_size("x")
    n_z = lax.axis_size("z")
    n_y = lax.axis_size("y")
    core = lax.axis_index("core").astype(jnp.int32)
    here = lax.axis_index(DOM)
    slots = slot_block.shape[0]
    n = coupling.shape[0]
    part = plane // groups
    width = planes * part
    n_locked = locked.shape[0]
    bands = groups * rows
    share_rows = n_locked // groups
    up, down = ring(domains)
    swap = [(0, 1), (1, 0)]

    x = orbitals.reshape(rows, cells)
    left = lax.ppermute(x, DOM, up)
    right = lax.ppermute(x, DOM, down)

    pot = potential.reshape(1, cells)
    weights = jnp.asarray(plane_weights(width_y))
    active = jnp.arange(slots, dtype=jnp.int32) < slot_count[0]
    relative = (slot_projector // n - here + domains) % domains
    section = jnp.where(relative == 0, 1, jnp.where(relative == 1, 2, 0))
    column = section * n + slot_projector % n
    column = jnp.where(active, column, BS)
    column = jnp.pad(column, (0, BS - slots), constant_values=BS)
    onehot = (column[:, None] == jnp.arange(BS, dtype=jnp.int32)[None, :]).astype(F32)
    coupling_row = jnp.pad(coupling[None], ((0, 0), (n, BS - 2 * n)))

    near = (here + domains + jnp.arange(-1, 2, dtype=jnp.int32)) % domains
    place = jnp.concatenate([near, jnp.stack([core, 1 - core, lax.axis_index("z"), 0, 0])])
    shares, place = pl.pallas_call(
        inner_kernel,
        out_shape=(
            jax.ShapeDtypeStruct((rows, BS), F32),
            jax.ShapeDtypeStruct((8,), jnp.int32),
        ),
        in_specs=[SMEM, SMEM, VMEM, VMEM, VMEM],
        out_specs=(VMEM, SMEM),
        compiler_params=params(8),
        cost_estimate=cost(2),
        name="inner",
    )(slot_block, place.astype(jnp.int32), x, projectors, onehot)
    below = lax.ppermute(shares, DOM, up)
    above = lax.ppermute(shares, DOM, down)

    h0, den = pl.pallas_call(
        functools.partial(local_kernel, planes),
        out_shape=(
            jax.ShapeDtypeStruct((rows, cells), F32),
            jax.ShapeDtypeStruct((rows, BS), F32),
        ),
        in_specs=[VMEM, VMEM, VMEM],
        out_specs=(VMEM, VMEM),
        scratch_shapes=[pltpu.VMEM((planes * rows, plane + 768), BF16)],
        compiler_params=params(24),
        cost_estimate=cost(7),
        name="local",
    )(x, pot, weights)

    hamilton, pay = pl.pallas_call(
        functools.partial(hamilton_kernel, planes),
        out_shape=(
            jax.ShapeDtypeStruct((rows, cells), F32),
            jax.ShapeDtypeStruct((domains, rows // 4 + 1, 1, BS), F32),
        ),
        in_specs=[VMEM] * 2 + [ANY] * 2 + [VMEM] * 3 + [ANY] * 2,
        out_specs=(VMEM, VMEM),
        scratch_shapes=[pltpu.VMEM((rows, cells), BF16)] * 2
        + [pltpu.VMEM((rows, BS), F32)] * 2
        + [pltpu.SemaphoreType.DMA((3, planes, 2)), pltpu.SemaphoreType.DMA((2,))],
        compiler_params=params(24),
        cost_estimate=cost(5),
        name="hamilton",
    )(h0, x, left, right, den, shares, coupling_row, below, above)
    pay = lax.all_to_all(pay, DOM, 0, 0, tiled=True)

    residual = pl.pallas_call(
        functools.partial(residual_kernel, planes),
        out_shape=jax.ShapeDtypeStruct((groups, rows, width), BF16),
        in_specs=[SMEM, SMEM, VMEM, VMEM, VMEM, ANY, ANY],
        out_specs=VMEM,
        scratch_shapes=[
            pltpu.VMEM((rows, cells), F32),
            pltpu.VMEM((slots, BS), F32),
            pltpu.VMEM((BS, BS), F32),
            pltpu.SemaphoreType.DMA((2,)),
        ],
        compiler_params=params(24),
        cost_estimate=cost(2),
        name="residual",
    )(slot_block, place, hamilton, x, pay, projectors, onehot)
    residual = lax.all_to_all(residual, BAND, 0, 0, tiled=True).reshape(bands, width)

    by_plane = locked.transpose(1, 0, 2).reshape(planes, n_x, 2, share_rows, part)
    by_plane = pltpu.with_memory_space_constraint(by_plane, pltpu.VMEM)

    def margin_call(side):
        return pl.pallas_call(
            functools.partial(margin_kernel, side),
            out_shape=jax.ShapeDtypeStruct((n_x, share_rows, bands), F32),
            in_specs=[SMEM, VMEM, VMEM],
            out_specs=VMEM,
            compiler_params=params(8),
            cost_estimate=cost(3),
            name="margin",
        )(place, by_plane, residual)

    given = lax.ppermute(margin_call(1), "core", swap)
    kept = margin_call(0)
    short = jax.ShapeDtypeStruct((n_x * n_y, n_z * 8, bands), BF16)
    share = pl.pallas_call(
        pair_kernel,
        out_shape=short,
        in_specs=[VMEM, VMEM],
        out_specs=VMEM,
        compiler_params=params(8),
        cost_estimate=cost(1),
        name="pair",
    )(kept, given)
    share = lax.all_to_all(share, SHORT, 0, 0, tiled=True)
    share = pl.pallas_call(
        partial_kernel,
        out_shape=jax.ShapeDtypeStruct((n_z, n_z * 8, bands), BF16),
        in_specs=[VMEM],
        out_specs=VMEM,
        compiler_params=params(8),
        cost_estimate=cost(1),
        name="partial",
    )(share)
    share = lax.all_to_all(share, "z", 0, 0, tiled=True)
    margins, coeffs = pl.pallas_call(
        total_kernel,
        out_shape=(jax.ShapeDtypeStruct((8, bands), F32), short),
        in_specs=[SMEM, VMEM],
        out_specs=(VMEM, VMEM),
        scratch_shapes=[pltpu.VMEM((n_z * 8, bands), F32)],
        compiler_params=params(8),
        cost_estimate=cost(1),
        name="total",
    )(place, share)
    coeffs = lax.all_to_all(coeffs, SHORT, 0, 0, tiled=True)
    other = lax.ppermute(coeffs, "core", swap)

    def clean_call(side, coeffs, before, kind):
        return pl.pallas_call(
            functools.partial(clean_kernel, side),
            out_shape=jax.ShapeDtypeStruct((planes, bands, part), kind),
            in_specs=[SMEM, VMEM, VMEM, VMEM],
            out_specs=VMEM,
            scratch_shapes=[pltpu.VMEM((n_x, bands, share_rows), BF16)],
            compiler_params=params(8),
            cost_estimate=cost(3),
            name="clean",
        )(place, by_plane, coeffs, before)

    part_clean = clean_call(0, coeffs, residual, F32)
    orthogonal = clean_call(1, other, part_clean, BF16)
    return orthogonal.transpose(1, 0, 2), margins


def solution(mesh):
    n_band, n_dom = mesh.devices.shape
    n_y = 4 if n_dom % 4 == 0 else 2
    fine = Mesh(
        mesh.devices.reshape(n_band // 2, 2, n_dom // n_y, n_y), ("x", "core", "z", "y")
    )
    in_specs = (
        P(BAND, DOM, None, None),
        P(DOM, None, None),
        P(DOM, None),
        P(DOM),
        P(DOM),
        P(DOM),
        P(DOM),
        P(None, DOM, BAND),
    )
    out_specs = (P(None, DOM, BAND), P(BAND + DOM, None))
    return jax.shard_map(
        per_device, mesh=fine, in_specs=in_specs, out_specs=out_specs, check_vma=False
    )
```

```python
import functools

import jax
import jax.numpy as jnp
import numpy as np
from jax import lax
from jax.experimental import pallas as pl
from jax.experimental.pallas import tpu as pltpu
from jax.sharding import Mesh
from jax.sharding import PartitionSpec as P

BS = 128

COEFFS = (
    -5369.0 / 1800.0,
    12.0 / 7.0,
    -15.0 / 56.0,
    10.0 / 189.0,
    -1.0 / 112.0,
    2.0 / 825.0,
    -1.0 / 5544.0,
)
HALF = tuple(-0.5 * c for c in COEFFS)
WIDTH = 6
DOM = ("z", "y")
BAND = ("x", "core")
SHORT = ("y", "x")
ENERGY = ("y", "z")
F32 = jnp.float32
BF16 = jnp.bfloat16
VMEM = pl.BlockSpec(memory_space=pltpu.VMEM)
SMEM = pl.BlockSpec(memory_space=pltpu.SMEM)
ANY = pl.BlockSpec(memory_space=pl.ANY)


def params(mib):
    return pltpu.CompilerParams(vmem_limit_bytes=mib * 1024 * 1024)


def cost(microseconds):
    return pl.CostEstimate(
        flops=0, transcendentals=0, bytes_accessed=int(microseconds * 3_000_000)
    )


@functools.lru_cache
def plane_weights(width_y):
    src = np.arange(1024)
    dst = np.arange(256)
    dz = np.abs((src // width_y - 2 * (384 // (2 * width_y)))[:, None] - (dst // width_y)[None])
    dy = np.abs((src % width_y)[:, None] - (dst % width_y)[None])
    dy = np.minimum(dy, width_y - dy)
    table = np.zeros(2048)
    table[1 : WIDTH + 1] = HALF[1:]
    full = np.where(dy == 0, table[dz], 0.0) + np.where(dz == 0, table[dy], 0.0)
    terms = []
    for _ in range(3):
        term = full.astype(np.float32).astype(BF16)
        terms.append(term)
        full = full - term.astype(np.float64)
    return np.stack(terms)


def inner_kernel(block_ref, place_ref, x_ref, proj_ref, onehot_ref, share_ref, out_ref):
    for i in range(out_ref.shape[0]):
        out_ref[i] = place_ref[i]
    rows = x_ref.shape[0]
    slots = proj_ref.shape[0]
    lane = lax.broadcasted_iota(jnp.int32, (rows, BS), 1)

    def body(s, acc):
        start = pl.multiple_of(block_ref[s] * BS, BS)
        cells = x_ref[:, pl.ds(start, BS)].astype(F32)
        total = jnp.sum(cells * proj_ref[pl.ds(s, 1), :], axis=1, keepdims=True)
        return jnp.where(lane == s, total, acc)

    acc = lax.fori_loop(0, slots, body, jnp.zeros((rows, BS), F32), unroll=8)
    share_ref[...] = jnp.dot(
        acc, onehot_ref[...], precision=lax.Precision.HIGHEST, preferred_element_type=F32
    )


def local_kernel(planes, x_ref, pot_ref, w_ref, out_ref, den_ref, pad_ref):
    rows = x_ref.shape[0]
    plane = x_ref.shape[1] // planes
    zeros = jnp.zeros((planes * rows, 384), BF16)
    pad_ref[:, :384] = zeros
    pad_ref[:, 384 + plane :] = zeros
    for p in range(planes):
        pad_ref[p * rows : (p + 1) * rows, 384 : 384 + plane] = x_ref[:, p * plane : (p + 1) * plane]

    def body(step, den):
        start = pl.multiple_of(step * 256, 256)
        window = pad_ref[:, pl.ds(start, 1024)]
        acc = jnp.dot(window, w_ref[0], preferred_element_type=F32)
        acc += jnp.dot(window, w_ref[1], preferred_element_type=F32)
        acc += jnp.dot(window, w_ref[2], preferred_element_type=F32)
        mid = [window[p * rows : (p + 1) * rows, 384:640].astype(F32) for p in range(planes)]
        for p in range(planes):
            where = pl.multiple_of(p * plane + start, 256)
            value = acc[p * rows : (p + 1) * rows]
            value += (pot_ref[:, pl.ds(where, 256)] + 3.0 * HALF[0]) * mid[p]
            for q in range(planes):
                if q != p and abs(q - p) <= WIDTH:
                    value += HALF[abs(q - p)] * mid[q]
            out_ref[:, pl.ds(where, 256)] = value
            square = mid[p] * mid[p]
            den += square[:, :BS] + square[:, BS:]
        return den

    den_ref[...] = lax.fori_loop(0, plane // 256, body, jnp.zeros((rows, BS), F32))


def hamilton_kernel(
    planes,
    h0_ref,
    x_ref,
    left_hbm,
    right_hbm,
    den_ref,
    mine_ref,
    coupling_ref,
    below_hbm,
    above_hbm,
    h_ref,
    pay_ref,
    left_ref,
    right_ref,
    below_ref,
    above_ref,
    sems,
    late_sems,
):
    rows, cells = x_ref.shape
    plane = cells // planes
    copies = []
    for i in range(rows // 16):
        pick = slice(i * 16, (i + 1) * 16)
        for j, (src, dst) in enumerate(((left_hbm, left_ref), (right_hbm, right_ref))):
            copies.append(pltpu.make_async_copy(src.at[pick], dst.at[pick], sems.at[i, j]))
    late = [
        pltpu.make_async_copy(below_hbm, below_ref, late_sems.at[0]),
        pltpu.make_async_copy(above_hbm, above_ref, late_sems.at[1]),
    ]
    for copy in copies + late:
        copy.start()
    n = BS // 4

    parts = []
    for i in range(rows // 16):
        pick = slice(i * 16, (i + 1) * 16)
        for copy in copies[2 * i : 2 * i + 2]:
            copy.wait()

        def halo(step, num, pick=pick):
            before = []
            after = []
            for p in range(planes):
                where = pl.ds(pl.multiple_of(p * plane + step * BS, BS), BS)
                before.append(left_ref[pick, where].astype(F32))
                after.append(right_ref[pick, where].astype(F32))
            for p in range(planes):
                where = pl.ds(pl.multiple_of(p * plane + step * BS, BS), BS)
                value = h0_ref[pick, where]
                for j in range(p, planes):
                    value += HALF[planes + p - j] * before[j]
                for j in range(p + 1):
                    value += HALF[planes + j - p] * after[j]
                h_ref[pick, where] = value
                num += value * x_ref[pick, where].astype(F32)
            return num

        parts.append(lax.fori_loop(0, plane // BS, halo, jnp.zeros((16, BS), F32), unroll=2))
    num = jnp.concatenate(parts, axis=0)

    for copy in late:
        copy.wait()
    lane = lax.broadcasted_iota(jnp.int32, (rows, BS), 1)
    row = lax.broadcasted_iota(jnp.int32, (rows, BS), 0)
    total = mine_ref[...]
    total += pltpu.roll(below_ref[...], 3 * n, 1)
    total += pltpu.roll(above_ref[...], n, 1)
    table = total * coupling_ref[...]
    num = jnp.sum(num + table * total, axis=1, keepdims=True)
    den = jnp.sum(den_ref[...], axis=1, keepdims=True)
    line = jnp.where(lane == row, num, 0.0) + jnp.where(lane == row + rows, den, 0.0)
    line = jnp.sum(line, axis=0, keepdims=True)

    short = rows // 4
    packed = None
    for g in range(4):
        piece = table[g * short : (g + 1) * short]
        piece = piece if g == 1 else pltpu.roll(piece, (g + 3) % 4 * n, 1)
        packed = piece if packed is None else packed + piece
    for r in range(short):
        pay_ref[:, r] = jnp.broadcast_to(packed[r : r + 1][None], (pay_ref.shape[0], 1, BS))
    pay_ref[:, short] = jnp.broadcast_to(line[None], (pay_ref.shape[0], 1, BS))


def residual_kernel(
    planes,
    block_ref,
    place_ref,
    h_ref,
    x_ref,
    pay_ref,
    proj_hbm,
    onehot_hbm,
    r_ref,
    full_ref,
    proj_ref,
    onehot_ref,
    sems,
):
    rows, cells = x_ref.shape
    plane = cells // planes
    late = [
        pltpu.make_async_copy(proj_hbm, proj_ref, sems.at[0]),
        pltpu.make_async_copy(onehot_hbm, onehot_ref, sems.at[1]),
    ]
    for copy in late:
        copy.start()
    slots = proj_ref.shape[0]
    n = BS // 4
    short = rows // 4
    lane = lax.broadcasted_iota(jnp.int32, (rows, BS), 1)
    row = lax.broadcasted_iota(jnp.int32, (rows, BS), 0)
    sums = jnp.sum(pay_ref[:, short], axis=0)
    num = jnp.sum(jnp.where(lane == row, sums, 0.0), axis=1, keepdims=True)
    den = jnp.sum(jnp.where(lane == row + rows, sums, 0.0), axis=1, keepdims=True)
    energy = jnp.broadcast_to(num / den, (rows, BS))
    for at in range(0, cells, BS):
        where = slice(at, at + BS)
        full_ref[:, where] = h_ref[:, where] - energy * x_ref[:, where].astype(F32)

    table = jnp.zeros((rows, BS), F32)
    for section in range(3):
        packed = jnp.concatenate(
            [pay_ref[place_ref[section], r] for r in range(short)], axis=0
        )
        pieces = [
            packed if g == section else pltpu.roll(packed, (section - g) % 4 * n, 1)
            for g in range(4)
        ]
        whole = jnp.concatenate(pieces, axis=0)
        table += jnp.where((lane >= section * n) & (lane < (section + 1) * n), whole, 0.0)
    for copy in late:
        copy.wait()
    value = lax.dot_general(
        table,
        onehot_ref[...],
        (((1,), (1,)), ((), ())),
        precision=lax.Precision.HIGHEST,
        preferred_element_type=F32,
    )
    for s in range(slots):
        where = pl.ds(pl.multiple_of(block_ref[s] * BS, BS), BS)
        full_ref[:, where] += value[:, s : s + 1] * proj_ref[s : s + 1, :]

    parts = r_ref.shape[0]
    part = plane // parts
    for c in range(parts):
        for p in range(planes):
            src = p * plane + c * part
            r_ref[c, :, p * part : (p + 1) * part] = full_ref[:, src : src + part].astype(BF16)


def margin_kernel(side, place_ref, locked_ref, r_ref, out_ref):
    planes, n_x, _, _, part = locked_ref.shape
    core = place_ref[3 + side]
    for i in range(n_x):
        acc = None
        for p in range(planes):
            term = lax.dot_general(
                locked_ref[p, i, core],
                r_ref[:, p * part : (p + 1) * part],
                (((1,), (1,)), ((), ())),
                preferred_element_type=F32,
            )
            acc = term if acc is None else acc + term
        out_ref[i] = acc


def pair_kernel(kept_ref, given_ref, out_ref):
    n_x, share_rows, _ = kept_ref.shape
    n_y = out_ref.shape[0] // n_x
    for i in range(n_x):
        for y in range(n_y):
            pieces = [
                kept_ref[i, at : at + 8] + given_ref[i, at : at + 8]
                for at in range(y * 8, share_rows, n_y * 8)
            ]
            out_ref[y * n_x + i] = jnp.concatenate(pieces, axis=0).astype(BF16)


def partial_kernel(in_ref, out_ref):
    acc = in_ref[0].astype(F32)
    for i in range(1, in_ref.shape[0]):
        acc += in_ref[i].astype(F32)
    value = acc.astype(BF16)
    for i in range(out_ref.shape[0]):
        out_ref[i] = value


def total_kernel(in_ref, total_ref, coeff_ref):
    acc = in_ref[0].astype(F32)
    for i in range(1, in_ref.shape[0]):
        acc += in_ref[i].astype(F32)
    total_ref[...] = acc
    value = acc.astype(BF16)
    for i in range(coeff_ref.shape[0]):
        coeff_ref[i] = value


def clean_kernel(side, place_ref, locked_ref, coeff_ref, r_ref, *refs):
    planes, n_x, _, share_rows, part = locked_ref.shape
    n_y = coeff_ref.shape[0] // n_x
    core = place_ref[3 + side]
    copies = []
    if side == 0:
        total_ref, out_ref, margin_hbm, turned_ref, sems = refs
        own = pl.ds(pl.multiple_of(place_ref[5] * 8, 8), 8)
        copies.append(pltpu.make_async_copy(total_ref.at[own], margin_hbm, sems.at[0]))
        copies[0].start()
    else:
        out_ref, turned_ref, stage_ref, sems = refs
    for i in range(n_x):
        pieces = [coeff_ref[y * n_x + i].astype(F32) for y in range(n_y)]
        whole = [
            pieces[at % n_y][at // n_y * 8 : at // n_y * 8 + 8] for at in range(share_rows // 8)
        ]
        turned_ref[i] = jnp.concatenate(whole, axis=0).astype(BF16).T
    for p in range(planes):
        term = None
        for i in range(n_x):
            more = jnp.dot(turned_ref[i], locked_ref[p, i, core], preferred_element_type=F32)
            term = more if term is None else term + more
        if side == 0:
            out_ref[p] = r_ref[:, p * part : (p + 1) * part].astype(F32) - term
        else:
            stage_ref[p] = (r_ref[p] - term).astype(BF16)
            copy = pltpu.make_async_copy(stage_ref.at[p], out_ref.at[p], sems.at[p])
            copy.start()
            copies.append(copy)
    for copy in copies:
        copy.wait()


def ring(size):
    up = [(i, (i + 1) % size) for i in range(size)]
    return up, [(j, i) for i, j in up]


def per_device(
    orbitals, potential, projectors, coupling, slot_block, slot_projector, slot_count, locked
):
    rows, planes, depth_z, width_y = orbitals.shape
    plane = depth_z * width_y
    cells = planes * plane
    domains = lax.axis_size(DOM)
    groups = lax.axis_size(BAND)
    n_x = lax.axis_size("x")
    n_z = lax.axis_size("z")
    n_y = lax.axis_size("y")
    core = lax.axis_index("core").astype(jnp.int32)
    here = lax.axis_index(DOM)
    slots = slot_block.shape[0]
    n = coupling.shape[0]
    part = plane // groups
    width = planes * part
    n_locked = locked.shape[0]
    bands = groups * rows
    share_rows = n_locked // groups
    up, down = ring(domains)
    swap = [(0, 1), (1, 0)]

    x = orbitals.reshape(rows, cells)
    left = lax.ppermute(x, DOM, up)
    right = lax.ppermute(x, DOM, down)

    pot = potential.reshape(1, cells)
    weights = jnp.asarray(plane_weights(width_y))
    active = jnp.arange(slots, dtype=jnp.int32) < slot_count[0]
    relative = (slot_projector // n - here + domains) % domains
    section = jnp.where(relative == 0, 1, jnp.where(relative == 1, 2, 0))
    column = section * n + slot_projector % n
    column = jnp.where(active, column, BS)
    column = jnp.pad(column, (0, BS - slots), constant_values=BS)
    onehot = (column[:, None] == jnp.arange(BS, dtype=jnp.int32)[None, :]).astype(F32)
    coupling_row = jnp.pad(coupling[None], ((0, 0), (n, BS - 2 * n)))

    near = (here + domains + jnp.arange(-1, 2, dtype=jnp.int32)) % domains
    near = near % n_y * n_z + near // n_y
    place = jnp.concatenate([near, jnp.stack([core, 1 - core, lax.axis_index("z"), 0, 0])])
    shares, place = pl.pallas_call(
        inner_kernel,
        out_shape=(
            jax.ShapeDtypeStruct((rows, BS), F32),
            jax.ShapeDtypeStruct((8,), jnp.int32),
        ),
        in_specs=[SMEM, SMEM, VMEM, VMEM, VMEM],
        out_specs=(VMEM, SMEM),
        compiler_params=params(8),
        cost_estimate=cost(2),
        name="inner",
    )(slot_block, place.astype(jnp.int32), x, projectors, onehot)
    below = lax.ppermute(shares, DOM, up)
    above = lax.ppermute(shares, DOM, down)

    h0, den = pl.pallas_call(
        functools.partial(local_kernel, planes),
        out_shape=(
            jax.ShapeDtypeStruct((rows, cells), F32),
            jax.ShapeDtypeStruct((rows, BS), F32),
        ),
        in_specs=[VMEM, VMEM, VMEM],
        out_specs=(VMEM, VMEM),
        scratch_shapes=[pltpu.VMEM((planes * rows, plane + 768), BF16)],
        compiler_params=params(24),
        cost_estimate=cost(7),
        name="local",
    )(x, pot, weights)

    hamilton, pay = pl.pallas_call(
        functools.partial(hamilton_kernel, planes),
        out_shape=(
            jax.ShapeDtypeStruct((rows, cells), F32),
            jax.ShapeDtypeStruct((domains, rows // 4 + 1, 1, BS), F32),
        ),
        in_specs=[VMEM] * 2 + [ANY] * 2 + [VMEM] * 3 + [ANY] * 2,
        out_specs=(VMEM, VMEM),
        scratch_shapes=[pltpu.VMEM((rows, cells), BF16)] * 2
        + [pltpu.VMEM((rows, BS), F32)] * 2
        + [pltpu.SemaphoreType.DMA((rows // 16, 2)), pltpu.SemaphoreType.DMA((2,))],
        compiler_params=params(24),
        cost_estimate=cost(5),
        name="hamilton",
    )(h0, x, left, right, den, shares, coupling_row, below, above)
    pay = lax.all_to_all(pay, ENERGY, 0, 0, tiled=True)

    residual = pl.pallas_call(
        functools.partial(residual_kernel, planes),
        out_shape=jax.ShapeDtypeStruct((groups, rows, width), BF16),
        in_specs=[SMEM, SMEM, VMEM, VMEM, VMEM, ANY, ANY],
        out_specs=VMEM,
        scratch_shapes=[
            pltpu.VMEM((rows, cells), F32),
            pltpu.VMEM((slots, BS), F32),
            pltpu.VMEM((BS, BS), F32),
            pltpu.SemaphoreType.DMA((2,)),
        ],
        compiler_params=params(24),
        cost_estimate=cost(2),
        name="residual",
    )(slot_block, place, hamilton, x, pay, projectors, onehot)
    residual = lax.all_to_all(residual, BAND, 0, 0, tiled=True).reshape(bands, width)

    by_plane = locked.transpose(1, 0, 2).reshape(planes, n_x, 2, share_rows, part)
    by_plane = pltpu.with_memory_space_constraint(by_plane, pltpu.VMEM)

    def margin_call(side):
        return pl.pallas_call(
            functools.partial(margin_kernel, side),
            out_shape=jax.ShapeDtypeStruct((n_x, share_rows, bands), F32),
            in_specs=[SMEM, VMEM, VMEM],
            out_specs=VMEM,
            compiler_params=params(8),
            cost_estimate=cost(3),
            name="margin",
        )(place, by_plane, residual)

    given = lax.ppermute(margin_call(1), "core", swap)
    kept = margin_call(0)
    short = jax.ShapeDtypeStruct((n_x * n_y, n_z * 8, bands), BF16)
    share = pl.pallas_call(
        pair_kernel,
        out_shape=short,
        in_specs=[VMEM, VMEM],
        out_specs=VMEM,
        compiler_params=params(8),
        cost_estimate=cost(1),
        name="pair",
    )(kept, given)
    share = lax.all_to_all(share, SHORT, 0, 0, tiled=True)
    share = pl.pallas_call(
        partial_kernel,
        out_shape=jax.ShapeDtypeStruct((n_z, n_z * 8, bands), BF16),
        in_specs=[VMEM],
        out_specs=VMEM,
        compiler_params=params(8),
        cost_estimate=cost(1),
        name="partial",
    )(share)
    share = lax.all_to_all(share, "z", 0, 0, tiled=True)
    total, coeffs = pl.pallas_call(
        total_kernel,
        out_shape=(jax.ShapeDtypeStruct((n_z * 8, bands), F32), short),
        in_specs=[VMEM],
        out_specs=(VMEM, VMEM),
        compiler_params=params(8),
        cost_estimate=cost(1),
        name="total",
    )(share)
    coeffs = lax.all_to_all(coeffs, SHORT, 0, 0, tiled=True)
    other = lax.ppermute(coeffs, "core", swap)

    def clean_call(side, *operands):
        made = jax.ShapeDtypeStruct((planes, bands, part), BF16 if side else F32)
        turned = pltpu.VMEM((n_x, bands, share_rows), BF16)
        stage = [pltpu.VMEM((planes, bands, part), BF16)] * side
        return pl.pallas_call(
            functools.partial(clean_kernel, side),
            out_shape=made if side else (made, jax.ShapeDtypeStruct((8, bands), F32)),
            in_specs=[SMEM] + [VMEM] * (len(operands) + 1),
            out_specs=ANY if side else (VMEM, ANY),
            scratch_shapes=[turned] + stage + [pltpu.SemaphoreType.DMA((planes,))],
            compiler_params=params(8),
            cost_estimate=cost(3),
            name="clean",
        )(place, by_plane, *operands)

    part_clean, margins = clean_call(0, coeffs, residual, total)
    orthogonal = clean_call(1, other, part_clean)
    return orthogonal.transpose(1, 0, 2), margins


def solution(mesh):
    n_band, n_dom = mesh.devices.shape
    n_y = 4 if n_dom % 4 == 0 else 2
    fine = Mesh(
        mesh.devices.reshape(n_band // 2, 2, n_dom // n_y, n_y), ("x", "core", "z", "y")
    )
    in_specs = (
        P(BAND, DOM, None, None),
        P(DOM, None, None),
        P(DOM, None),
        P(DOM),
        P(DOM),
        P(DOM),
        P(DOM),
        P(None, DOM, BAND),
    )
    out_specs = (P(None, DOM, BAND), P(BAND + DOM, None))
    return jax.shard_map(
        per_device, mesh=fine, in_specs=in_specs, out_specs=out_specs, check_vma=False
    )
```

```python
import functools

import jax
import jax.numpy as jnp
import numpy as np
from jax import lax
from jax.experimental import pallas as pl
from jax.experimental.pallas import tpu as pltpu
from jax.sharding import Mesh
from jax.sharding import PartitionSpec as P

BS = 128

COEFFS = (
    -5369.0 / 1800.0,
    12.0 / 7.0,
    -15.0 / 56.0,
    10.0 / 189.0,
    -1.0 / 112.0,
    2.0 / 825.0,
    -1.0 / 5544.0,
)
HALF = tuple(-0.5 * c for c in COEFFS)
WIDTH = 6
DOM = ("z", "y")
BAND = ("x", "core")
SHORT = ("x", "y")
SPREAD = ("y", "x")
ENERGY = ("y", "z")
F32 = jnp.float32
BF16 = jnp.bfloat16
VMEM = pl.BlockSpec(memory_space=pltpu.VMEM)
SMEM = pl.BlockSpec(memory_space=pltpu.SMEM)
ANY = pl.BlockSpec(memory_space=pl.ANY)


def params(mib):
    return pltpu.CompilerParams(vmem_limit_bytes=mib * 1024 * 1024)


def cost(microseconds):
    return pl.CostEstimate(
        flops=0, transcendentals=0, bytes_accessed=int(microseconds * 3_000_000)
    )


@functools.lru_cache
def plane_weights(width_y):
    src = np.arange(1024)
    dst = np.arange(256)
    dz = np.abs((src // width_y - 2 * (384 // (2 * width_y)))[:, None] - (dst // width_y)[None])
    dy = np.abs((src % width_y)[:, None] - (dst % width_y)[None])
    dy = np.minimum(dy, width_y - dy)
    table = np.zeros(2048)
    table[1 : WIDTH + 1] = HALF[1:]
    full = np.where(dy == 0, table[dz], 0.0) + np.where(dz == 0, table[dy], 0.0)
    terms = []
    for _ in range(3):
        term = full.astype(np.float32).astype(BF16)
        terms.append(term)
        full = full - term.astype(np.float64)
    return np.stack(terms)


def inner_kernel(block_ref, place_ref, x_ref, proj_ref, onehot_ref, share_ref, out_ref):
    for i in range(out_ref.shape[0]):
        out_ref[i] = place_ref[i]
    rows = x_ref.shape[0]
    slots = proj_ref.shape[0]
    lane = lax.broadcasted_iota(jnp.int32, (rows, BS), 1)

    def body(s, acc):
        start = pl.multiple_of(block_ref[s] * BS, BS)
        cells = x_ref[:, pl.ds(start, BS)].astype(F32)
        total = jnp.sum(cells * proj_ref[pl.ds(s, 1), :], axis=1, keepdims=True)
        return jnp.where(lane == s, total, acc)

    acc = lax.fori_loop(0, slots, body, jnp.zeros((rows, BS), F32), unroll=8)
    share_ref[...] = jnp.dot(
        acc, onehot_ref[...], precision=lax.Precision.HIGHEST, preferred_element_type=F32
    )


def local_kernel(planes, x_ref, pot_ref, w_ref, out_ref, den_ref, pad_ref):
    rows = x_ref.shape[0]
    plane = x_ref.shape[1] // planes
    zeros = jnp.zeros((planes * rows, 384), BF16)
    pad_ref[:, :384] = zeros
    pad_ref[:, 384 + plane :] = zeros
    for p in range(planes):
        pad_ref[p * rows : (p + 1) * rows, 384 : 384 + plane] = x_ref[:, p * plane : (p + 1) * plane]

    def body(step, den):
        start = pl.multiple_of(step * 256, 256)
        window = pad_ref[:, pl.ds(start, 1024)]
        acc = jnp.dot(window, w_ref[0], preferred_element_type=F32)
        acc += jnp.dot(window, w_ref[1], preferred_element_type=F32)
        acc += jnp.dot(window, w_ref[2], preferred_element_type=F32)
        mid = [window[p * rows : (p + 1) * rows, 384:640].astype(F32) for p in range(planes)]
        for p in range(planes):
            where = pl.multiple_of(p * plane + start, 256)
            value = acc[p * rows : (p + 1) * rows]
            value += (pot_ref[:, pl.ds(where, 256)] + 3.0 * HALF[0]) * mid[p]
            for q in range(planes):
                if q != p and abs(q - p) <= WIDTH:
                    value += HALF[abs(q - p)] * mid[q]
            out_ref[:, pl.ds(where, 256)] = value
            square = mid[p] * mid[p]
            den += square[:, :BS] + square[:, BS:]
        return den

    den_ref[...] = lax.fori_loop(0, plane // 256, body, jnp.zeros((rows, BS), F32))


def hamilton_kernel(
    planes,
    h0_ref,
    x_ref,
    left_hbm,
    right_hbm,
    den_ref,
    mine_ref,
    coupling_ref,
    below_hbm,
    above_hbm,
    h_ref,
    pay_ref,
    left_ref,
    right_ref,
    below_ref,
    above_ref,
    sems,
    late_sems,
):
    rows, cells = x_ref.shape
    plane = cells // planes
    copies = []
    for i in range(rows // 16):
        pick = slice(i * 16, (i + 1) * 16)
        for j, (src, dst) in enumerate(((left_hbm, left_ref), (right_hbm, right_ref))):
            copies.append(pltpu.make_async_copy(src.at[pick], dst.at[pick], sems.at[i, j]))
    late = [
        pltpu.make_async_copy(below_hbm, below_ref, late_sems.at[0]),
        pltpu.make_async_copy(above_hbm, above_ref, late_sems.at[1]),
    ]
    for copy in copies + late:
        copy.start()
    n = BS // 4

    parts = []
    for i in range(rows // 16):
        pick = slice(i * 16, (i + 1) * 16)
        for copy in copies[2 * i : 2 * i + 2]:
            copy.wait()

        def halo(step, num, pick=pick):
            before = []
            after = []
            for p in range(planes):
                where = pl.ds(pl.multiple_of(p * plane + step * BS, BS), BS)
                before.append(left_ref[pick, where].astype(F32))
                after.append(right_ref[pick, where].astype(F32))
            for p in range(planes):
                where = pl.ds(pl.multiple_of(p * plane + step * BS, BS), BS)
                value = h0_ref[pick, where]
                for j in range(p, planes):
                    value += HALF[planes + p - j] * before[j]
                for j in range(p + 1):
                    value += HALF[planes + j - p] * after[j]
                h_ref[pick, where] = value
                num += value * x_ref[pick, where].astype(F32)
            return num

        parts.append(lax.fori_loop(0, plane // BS, halo, jnp.zeros((16, BS), F32), unroll=4))
    num = jnp.concatenate(parts, axis=0)

    for copy in late:
        copy.wait()
    lane = lax.broadcasted_iota(jnp.int32, (rows, BS), 1)
    row = lax.broadcasted_iota(jnp.int32, (rows, BS), 0)
    total = mine_ref[...]
    total += pltpu.roll(below_ref[...], 3 * n, 1)
    total += pltpu.roll(above_ref[...], n, 1)
    table = total * coupling_ref[...]
    num = jnp.sum(num + table * total, axis=1, keepdims=True)
    den = jnp.sum(den_ref[...], axis=1, keepdims=True)
    line = jnp.where(lane == row, num, 0.0) + jnp.where(lane == row + rows, den, 0.0)
    line = jnp.sum(line, axis=0, keepdims=True)

    short = rows // 4
    packed = None
    for g in range(4):
        piece = table[g * short : (g + 1) * short]
        piece = piece if g == 1 else pltpu.roll(piece, (g + 3) % 4 * n, 1)
        packed = piece if packed is None else packed + piece
    for r in range(short):
        pay_ref[:, r] = jnp.broadcast_to(packed[r : r + 1][None], (pay_ref.shape[0], 1, BS))
    pay_ref[:, short] = jnp.broadcast_to(line[None], (pay_ref.shape[0], 1, BS))


def residual_kernel(
    planes,
    block_ref,
    place_ref,
    h_ref,
    x_ref,
    pay_ref,
    proj_hbm,
    onehot_hbm,
    r_ref,
    full_ref,
    proj_ref,
    onehot_ref,
    sems,
):
    rows, cells = x_ref.shape
    plane = cells // planes
    late = [
        pltpu.make_async_copy(proj_hbm, proj_ref, sems.at[0]),
        pltpu.make_async_copy(onehot_hbm, onehot_ref, sems.at[1]),
    ]
    for copy in late:
        copy.start()
    slots = proj_ref.shape[0]
    n = BS // 4
    short = rows // 4
    lane = lax.broadcasted_iota(jnp.int32, (rows, BS), 1)
    row = lax.broadcasted_iota(jnp.int32, (rows, BS), 0)
    sums = jnp.sum(pay_ref[:, short], axis=0)
    num = jnp.sum(jnp.where(lane == row, sums, 0.0), axis=1, keepdims=True)
    den = jnp.sum(jnp.where(lane == row + rows, sums, 0.0), axis=1, keepdims=True)
    energy = jnp.broadcast_to(num / den, (rows, BS))
    for at in range(0, cells, BS):
        where = slice(at, at + BS)
        full_ref[:, where] = h_ref[:, where] - energy * x_ref[:, where].astype(F32)

    table = jnp.zeros((rows, BS), F32)
    for section in range(3):
        packed = jnp.concatenate(
            [pay_ref[place_ref[section], r] for r in range(short)], axis=0
        )
        pieces = [
            packed if g == section else pltpu.roll(packed, (section - g) % 4 * n, 1)
            for g in range(4)
        ]
        whole = jnp.concatenate(pieces, axis=0)
        table += jnp.where((lane >= section * n) & (lane < (section + 1) * n), whole, 0.0)
    for copy in late:
        copy.wait()
    value = lax.dot_general(
        table,
        onehot_ref[...],
        (((1,), (1,)), ((), ())),
        precision=lax.Precision.HIGHEST,
        preferred_element_type=F32,
    )
    for s in range(slots):
        where = pl.ds(pl.multiple_of(block_ref[s] * BS, BS), BS)
        full_ref[:, where] += value[:, s : s + 1] * proj_ref[s : s + 1, :]

    parts = r_ref.shape[0]
    part = plane // parts
    for c in range(parts):
        for p in range(planes):
            src = p * plane + c * part
            r_ref[c, :, p * part : (p + 1) * part] = full_ref[:, src : src + part].astype(BF16)


def margin_kernel(side, place_ref, locked_ref, r_ref, out_ref):
    planes, n_x, _, _, part = locked_ref.shape
    core = place_ref[3 + side]
    for i in range(n_x):
        acc = None
        for p in range(planes):
            term = lax.dot_general(
                locked_ref[p, i, core],
                r_ref[:, p * part : (p + 1) * part],
                (((1,), (1,)), ((), ())),
                preferred_element_type=F32,
            )
            acc = term if acc is None else acc + term
        out_ref[i] = acc


def pair_kernel(kept_ref, given_ref, out_ref):
    n_x, share_rows, _ = kept_ref.shape
    n_y = out_ref.shape[0] // n_x
    for i in range(n_x):
        for y in range(n_y):
            pieces = [
                kept_ref[i, at : at + 8] + given_ref[i, at : at + 8]
                for at in range(y * 8, share_rows, n_y * 8)
            ]
            out_ref[i * n_y + y] = jnp.concatenate(pieces, axis=0).astype(BF16)


def partial_kernel(in_ref, out_ref):
    acc = in_ref[0].astype(F32)
    for i in range(1, in_ref.shape[0]):
        acc += in_ref[i].astype(F32)
    value = acc.astype(BF16)
    for i in range(out_ref.shape[0]):
        out_ref[i] = value


def total_kernel(in_ref, total_ref, coeff_ref):
    acc = in_ref[0].astype(F32)
    for i in range(1, in_ref.shape[0]):
        acc += in_ref[i].astype(F32)
    total_ref[...] = acc
    value = acc.astype(BF16)
    for i in range(coeff_ref.shape[0]):
        coeff_ref[i] = value


def clean_kernel(side, place_ref, locked_ref, coeff_ref, r_ref, *refs):
    planes, n_x, _, share_rows, part = locked_ref.shape
    n_y = coeff_ref.shape[0] // n_x
    core = place_ref[3 + side]
    copies = []
    if side == 0:
        total_ref, out_ref, margin_hbm, turned_ref, sems = refs
        own = pl.ds(pl.multiple_of(place_ref[5] * 8, 8), 8)
        copies.append(pltpu.make_async_copy(total_ref.at[own], margin_hbm, sems.at[0]))
        copies[0].start()
    else:
        out_ref, turned_ref, stage_ref, sems = refs
    for i in range(n_x):
        pieces = [coeff_ref[y * n_x + i].astype(F32) for y in range(n_y)]
        whole = [
            pieces[at % n_y][at // n_y * 8 : at // n_y * 8 + 8] for at in range(share_rows // 8)
        ]
        turned_ref[i] = jnp.concatenate(whole, axis=0).astype(BF16).T
    for p in range(planes):
        term = None
        for i in range(n_x):
            more = jnp.dot(turned_ref[i], locked_ref[p, i, core], preferred_element_type=F32)
            term = more if term is None else term + more
        if side == 0:
            out_ref[p] = r_ref[:, p * part : (p + 1) * part].astype(F32) - term
        else:
            stage_ref[p] = (r_ref[p] - term).astype(BF16)
            copy = pltpu.make_async_copy(stage_ref.at[p], out_ref.at[p], sems.at[p])
            copy.start()
            copies.append(copy)
    for copy in copies:
        copy.wait()


def ring(size):
    up = [(i, (i + 1) % size) for i in range(size)]
    return up, [(j, i) for i, j in up]


def per_device(
    orbitals, potential, projectors, coupling, slot_block, slot_projector, slot_count, locked
):
    rows, planes, depth_z, width_y = orbitals.shape
    plane = depth_z * width_y
    cells = planes * plane
    domains = lax.axis_size(DOM)
    groups = lax.axis_size(BAND)
    n_x = lax.axis_size("x")
    n_z = lax.axis_size("z")
    n_y = lax.axis_size("y")
    core = lax.axis_index("core").astype(jnp.int32)
    here = lax.axis_index(DOM)
    slots = slot_block.shape[0]
    n = coupling.shape[0]
    part = plane // groups
    width = planes * part
    n_locked = locked.shape[0]
    bands = groups * rows
    share_rows = n_locked // groups
    up, down = ring(domains)
    swap = [(0, 1), (1, 0)]

    x = orbitals.reshape(rows, cells)
    left = lax.ppermute(x, DOM, up)
    right = lax.ppermute(x, DOM, down)

    pot = potential.reshape(1, cells)
    weights = jnp.asarray(plane_weights(width_y))
    active = jnp.arange(slots, dtype=jnp.int32) < slot_count[0]
    relative = (slot_projector // n - here + domains) % domains
    section = jnp.where(relative == 0, 1, jnp.where(relative == 1, 2, 0))
    column = section * n + slot_projector % n
    column = jnp.where(active, column, BS)
    column = jnp.pad(column, (0, BS - slots), constant_values=BS)
    onehot = (column[:, None] == jnp.arange(BS, dtype=jnp.int32)[None, :]).astype(F32)
    coupling_row = jnp.pad(coupling[None], ((0, 0), (n, BS - 2 * n)))

    near = (here + domains + jnp.arange(-1, 2, dtype=jnp.int32)) % domains
    near = near % n_y * n_z + near // n_y
    place = jnp.concatenate([near, jnp.stack([core, 1 - core, lax.axis_index("z"), 0, 0])])
    shares, place = pl.pallas_call(
        inner_kernel,
        out_shape=(
            jax.ShapeDtypeStruct((rows, BS), F32),
            jax.ShapeDtypeStruct((8,), jnp.int32),
        ),
        in_specs=[SMEM, SMEM, VMEM, VMEM, VMEM],
        out_specs=(VMEM, SMEM),
        compiler_params=params(8),
        cost_estimate=cost(2),
        name="inner",
    )(slot_block, place.astype(jnp.int32), x, projectors, onehot)
    below = lax.ppermute(shares, DOM, up)
    above = lax.ppermute(shares, DOM, down)

    h0, den = pl.pallas_call(
        functools.partial(local_kernel, planes),
        out_shape=(
            jax.ShapeDtypeStruct((rows, cells), F32),
            jax.ShapeDtypeStruct((rows, BS), F32),
        ),
        in_specs=[VMEM, VMEM, VMEM],
        out_specs=(VMEM, VMEM),
        scratch_shapes=[pltpu.VMEM((planes * rows, plane + 768), BF16)],
        compiler_params=params(24),
        cost_estimate=cost(7),
        name="local",
    )(x, pot, weights)

    hamilton, pay = pl.pallas_call(
        functools.partial(hamilton_kernel, planes),
        out_shape=(
            jax.ShapeDtypeStruct((rows, cells), F32),
            jax.ShapeDtypeStruct((domains, rows // 4 + 1, 1, BS), F32),
        ),
        in_specs=[VMEM] * 2 + [ANY] * 2 + [VMEM] * 3 + [ANY] * 2,
        out_specs=(VMEM, VMEM),
        scratch_shapes=[pltpu.VMEM((rows, cells), BF16)] * 2
        + [pltpu.VMEM((rows, BS), F32)] * 2
        + [pltpu.SemaphoreType.DMA((rows // 16, 2)), pltpu.SemaphoreType.DMA((2,))],
        compiler_params=params(24),
        cost_estimate=cost(5),
        name="hamilton",
    )(h0, x, left, right, den, shares, coupling_row, below, above)
    pay = lax.all_to_all(pay, ENERGY, 0, 0, tiled=True)

    residual = pl.pallas_call(
        functools.partial(residual_kernel, planes),
        out_shape=jax.ShapeDtypeStruct((groups, rows, width), BF16),
        in_specs=[SMEM, SMEM, VMEM, VMEM, VMEM, ANY, ANY],
        out_specs=VMEM,
        scratch_shapes=[
            pltpu.VMEM((rows, cells), F32),
            pltpu.VMEM((slots, BS), F32),
            pltpu.VMEM((BS, BS), F32),
            pltpu.SemaphoreType.DMA((2,)),
        ],
        compiler_params=params(24),
        cost_estimate=cost(2),
        name="residual",
    )(slot_block, place, hamilton, x, pay, projectors, onehot)
    residual = lax.all_to_all(residual, BAND, 0, 0, tiled=True).reshape(bands, width)

    by_plane = locked.transpose(1, 0, 2).reshape(planes, n_x, 2, share_rows, part)
    by_plane = pltpu.with_memory_space_constraint(by_plane, pltpu.VMEM)

    def margin_call(side):
        return pl.pallas_call(
            functools.partial(margin_kernel, side),
            out_shape=jax.ShapeDtypeStruct((n_x, share_rows, bands), F32),
            in_specs=[SMEM, VMEM, VMEM],
            out_specs=VMEM,
            compiler_params=params(8),
            cost_estimate=cost(3),
            name="margin",
        )(place, by_plane, residual)

    given = lax.ppermute(margin_call(1), "core", swap)
    kept = margin_call(0)
    short = jax.ShapeDtypeStruct((n_x * n_y, n_z * 8, bands), BF16)
    share = pl.pallas_call(
        pair_kernel,
        out_shape=short,
        in_specs=[VMEM, VMEM],
        out_specs=VMEM,
        compiler_params=params(8),
        cost_estimate=cost(1),
        name="pair",
    )(kept, given)
    share = lax.all_to_all(share, SHORT, 0, 0, tiled=True)
    share = pl.pallas_call(
        partial_kernel,
        out_shape=jax.ShapeDtypeStruct((n_z, n_z * 8, bands), BF16),
        in_specs=[VMEM],
        out_specs=VMEM,
        compiler_params=params(8),
        cost_estimate=cost(1),
        name="partial",
    )(share)
    share = lax.all_to_all(share, "z", 0, 0, tiled=True)
    total, coeffs = pl.pallas_call(
        total_kernel,
        out_shape=(jax.ShapeDtypeStruct((n_z * 8, bands), F32), short),
        in_specs=[VMEM],
        out_specs=(VMEM, VMEM),
        compiler_params=params(8),
        cost_estimate=cost(1),
        name="total",
    )(share)
    coeffs = lax.all_to_all(coeffs, SPREAD, 0, 0, tiled=True)
    other = lax.ppermute(coeffs, "core", swap)

    def clean_call(side, *operands):
        made = jax.ShapeDtypeStruct((planes, bands, part), BF16 if side else F32)
        turned = pltpu.VMEM((n_x, bands, share_rows), BF16)
        stage = [pltpu.VMEM((planes, bands, part), BF16)] * side
        return pl.pallas_call(
            functools.partial(clean_kernel, side),
            out_shape=made if side else (made, jax.ShapeDtypeStruct((8, bands), F32)),
            in_specs=[SMEM] + [VMEM] * (len(operands) + 1),
            out_specs=ANY if side else (VMEM, ANY),
            scratch_shapes=[turned] + stage + [pltpu.SemaphoreType.DMA((planes,))],
            compiler_params=params(8),
            cost_estimate=cost(3),
            name="clean",
        )(place, by_plane, *operands)

    part_clean, margins = clean_call(0, coeffs, residual, total)
    orthogonal = clean_call(1, other, part_clean)
    return orthogonal.transpose(1, 0, 2), margins


def solution(mesh):
    n_band, n_dom = mesh.devices.shape
    n_y = 4 if n_dom % 4 == 0 else 2
    fine = Mesh(
        mesh.devices.reshape(n_band // 2, 2, n_dom // n_y, n_y), ("x", "core", "z", "y")
    )
    in_specs = (
        P(BAND, DOM, None, None),
        P(DOM, None, None),
        P(DOM, None),
        P(DOM),
        P(DOM),
        P(DOM),
        P(DOM),
        P(None, DOM, BAND),
    )
    out_specs = (P(None, DOM, BAND), P(BAND + DOM, None))
    return jax.shard_map(
        per_device, mesh=fine, in_specs=in_specs, out_specs=out_specs, check_vma=False
    )
```
